512 devices in a mesh: feat: 16 (over z), batch: 32 (over y, x, core).
Axes of the slice: x: 4, y: 4, z: 16, core: 2. Of those that a mesh axis runs over, the one named last changes fastest.
Arguments:
- feats: bfloat16 [32, 768, 8192], P('batch', 'feat'), may hold values from -6 to 6
- nbr_one: int32 [32, 15, 1024], P('batch'), may hold values from 0 to 8191
- rel_one: int32 [32, 15, 1024], P('batch'), may hold values from 0 to 4
- w_one: bfloat16 [5, 768, 1024], P(None, 'feat'), may hold values from -0.09375 to 0.09375
- owner_two: int32 [32, 1024, 10, 1], P('batch'), may hold values from 0 to 31; in each aligned block of 640 rows (0 to 639, 640 to 1279, ..., all dimensions but the last counted through in order) at most 40 rows name the same one
- local_two: int32 [32, 1024, 10], P('batch'), may hold values from 0 to 63
- rel_two: int32 [32, 1024, 10], P('batch'), may hold values from 0 to 4
- w_two: bfloat16 [5, 1024, 1024], P(None, 'feat'), may hold values from -0.078125 to 0.078125
Outputs:
- hidden_two: bfloat16 [32, 1024, 1024], P('batch', 'feat')
The draws below stay inside these ranges and needn't reach their ends.
Inputs may be any that keep to these rules, and one draw needn't show every extreme that they name: `owner_two`: every neighbour of destination j lies in the block of rows (j // 64) * 64 to (j // 64) * 64 + 63 of its mini-batch; among the 640 edges of each aligned block of 64 destinations, no mini-batch is named more than 40 times. `rel_one`: the value 4 marks an empty slot. `rel_two`: the value 4 marks an empty slot.
All inputs are finite; a program needn't handle non-finite values.
Results may differ from the reference program's by a relative error of at most 0.025.
Values may be sent and summed in bfloat16 or wider, within the bound.
A program may use at most 64 MiB of HBM per device.

```python
import math
import jax
import jax.numpy as jnp
import numpy as np
from jax import lax

FEAT_IN = 768
HIDDEN_SIZE = 1024
RELATIONS = 4
FANOUT_ONE = 15
FANOUT_TWO = 10
ROWS = 64
BATCHES = 32
DEST = 1024
SOURCES = 8192
CAP = 40
N_FEAT = 16
N_BATCH = 32


def set_ends(array, own_key, least, high):
    place = [jax.random.randint(jax.random.fold_in(own_key, axis), (), 0, length) for axis, length in enumerate(array.shape)]
    longest = array.shape.index(max(array.shape))
    neighbour = place[:longest] + [(place[longest] + 1) % array.shape[longest]] + place[longest + 1:]
    return array.at[tuple(place)].set(least).at[tuple(neighbour)].set(high)


def block_scale(stream_key, shape, shards, least, largest):
    def one(position, parts):
        draws = jax.random.uniform(jax.random.fold_in(jax.random.fold_in(stream_key, 6), position), (parts,), jnp.float32, least / len(shards), largest / len(shards))
        return jnp.repeat(jnp.exp(draws), shape[position] // parts).reshape((-1,) + (1,) * (len(shape) - position - 1))

    loudness = one(*shards[0])
    for cut in shards[1:]:
        loudness = loudness * one(*cut)
    return loudness


def routed_block(key, own, number, rows, number_of, top, limit, lean):
    order = jax.random.permutation(key, number_of)
    packed, usual = portions_of(number_of, rows * top, limit, lean, True), portions_of(number_of, rows * top, limit, lean, False)
    places = jnp.arange(number_of)

    def named(lengths, rotation):
        used = int((lengths > 0).sum())
        fixed = max(1, used // 4)
        shifted = fixed + (places - fixed + rotation * (used - fixed)) % max(1, number_of - fixed)
        return jnp.zeros((number_of,), jnp.int32).at[order[jnp.where(places < fixed, places, shifted)]].set(jnp.asarray(lengths, jnp.int32))

    lengths = jnp.where(number % 4 == 0, named(packed, number // 4), named(usual, number - number // 4 - 1))
    mixed = jax.random.permutation(jax.random.fold_in(own, 3), number_of)
    source_of, receiver = mixed[0:number_of // 2 * 2:2], mixed[1:number_of // 2 * 2:2]
    room = jnp.minimum(lengths[source_of] - 1, limit - lengths[receiver]) // 2
    room = jnp.where((source_of == order[0]) | (receiver == order[0]) | (lengths[receiver] == 0), 0, jnp.maximum(room, 0))
    shifted = jax.random.randint(jax.random.fold_in(own, 4), (number_of // 2,), 0, 1 << 20) % (room + 1)
    lengths = lengths.at[source_of].add(-shifted).at[receiver].add(shifted)
    items = jnp.searchsorted(jnp.cumsum(lengths), jnp.arange(rows * top), side="right").astype(jnp.int32)
    table = items.reshape(top, rows).T
    table = table[jax.random.permutation(jax.random.fold_in(own, 1), rows)]
    rotation = jax.random.randint(jax.random.fold_in(own, 2), (rows, 1), 0, top)
    return jnp.take_along_axis(table, (jnp.arange(top)[None, :] + rotation) % top, axis=1)


def portions_of(number_of, total, limit, lean, full):
    loads = [(1 << 20) // math.isqrt(rank ** lean) + 1 for rank in range(1, number_of + 1)]
    largest = limit if full else min(limit, max(-(-total // number_of), total * loads[0] // sum(loads)))
    least = 1 if total - largest >= number_of - 1 else 0
    holding, rest = [largest] + [least] * (number_of - 1), total - largest - least * (number_of - 1)
    while rest > 0:
        free = [i for i in range(1, number_of) if holding[i] < largest] or [i for i in range(1, number_of) if holding[i] < limit]
        pool, left = sum([loads[i] for i in free]), rest
        for i in free:
            addition = min(limit - holding[i], max(1, left * loads[i] // pool), rest)
            holding[i] = holding[i] + addition
            rest = rest - addition
    return np.array(holding)


def noise(stream_key, extent, deviation, reach, pieces=(), kind=jnp.bfloat16):
    array = deviation * jax.random.normal(stream_key, extent, jnp.float32)
    if pieces:
        array = array * block_scale(stream_key, extent, pieces, -0.22, 0.18)
    return jnp.clip(array, -reach, reach).astype(kind)


def setup_inputs(seed: int = 0) -> dict:
    streams_of = jax.random.split(jax.random.key(seed), 9)
    feats = noise(streams_of[0], (BATCHES, FEAT_IN, SOURCES), 1.0, 6.0, ((0, 32), (1, 16)))
    nbr_one = set_ends(jax.random.randint(streams_of[1], (BATCHES, FANOUT_ONE, DEST), 0, SOURCES), jax.random.fold_in(streams_of[1], 1), 0, SOURCES - 1).astype(jnp.int32)
    rel_one = set_ends(jax.random.randint(streams_of[2], (BATCHES, FANOUT_ONE, DEST), 0, RELATIONS + 1), jax.random.fold_in(streams_of[2], 1), 0, RELATIONS).astype(jnp.int32)
    w_one = noise(streams_of[3], (RELATIONS + 1, FEAT_IN, HIDDEN_SIZE), (FEAT_IN * (RELATIONS + 1)) ** -0.5, 0.09375, ((1, 16),))
    owner_two_keys = jax.random.split(jax.random.fold_in(streams_of[4], 1), BATCHES * DEST * FANOUT_TWO // (ROWS * FANOUT_TWO))
    owner_two_turns = jax.random.permutation(jax.random.fold_in(streams_of[4], 3), BATCHES * DEST * FANOUT_TWO // (ROWS * FANOUT_TWO))
    owner_two = jax.vmap(lambda own, number: routed_block(jax.random.fold_in(streams_of[4], 2), own, number, ROWS * FANOUT_TWO, N_BATCH, 1, CAP, 2))(owner_two_keys, owner_two_turns).reshape((BATCHES, DEST, FANOUT_TWO, 1))
    local_two = set_ends(jax.random.randint(streams_of[5], (BATCHES, DEST, FANOUT_TWO), 0, ROWS), jax.random.fold_in(streams_of[5], 1), 0, ROWS - 1).astype(jnp.int32)
    rel_two = set_ends(jax.random.randint(streams_of[6], (BATCHES, DEST, FANOUT_TWO), 0, RELATIONS + 1), jax.random.fold_in(streams_of[6], 1), 0, RELATIONS).astype(jnp.int32)
    w_two = noise(streams_of[7], (RELATIONS + 1, HIDDEN_SIZE, HIDDEN_SIZE), (HIDDEN_SIZE * (RELATIONS + 1)) ** -0.5, 0.078125, ((1, 16),))
    return dict(feats=feats, nbr_one=nbr_one, rel_one=rel_one, w_one=w_one, owner_two=owner_two, local_two=local_two, rel_two=rel_two, w_two=w_two)


def relation_means(picked, relation_ids, own_rows, widen_at, along_picked, along_ids):
    slabs = [own_rows]
    for relation in range(RELATIONS):
        chosen = relation_ids == relation
        counter = jnp.maximum(jnp.sum(chosen.astype(jnp.int32), axis=along_ids), 1).astype(jnp.float32)
        summed = jnp.sum(jnp.where(jnp.expand_dims(chosen, widen_at), picked, jnp.zeros((), picked.dtype)), axis=along_picked, dtype=jnp.float32)
        slabs.append((summed / jnp.expand_dims(counter, widen_at)).astype(jnp.bfloat16))
    return jnp.stack(slabs)


def reference(feats, nbr_one, rel_one, w_one, owner_two, local_two, rel_two, w_two):
    weights_one = w_one.astype(jnp.float32).reshape(RELATIONS + 1, N_FEAT, FEAT_IN // N_FEAT, HIDDEN_SIZE)
    weights_two = w_two.astype(jnp.float32).reshape(RELATIONS + 1, N_FEAT, HIDDEN_SIZE // N_FEAT, HIDDEN_SIZE)

    def first_layer(operands):
        columns, neighbours, relation_ids = operands
        picked = jnp.take(columns, neighbours, axis=1)
        slabs = relation_means(picked, relation_ids, columns[:, :DEST], 0, 1, 0)
        inputs = lax.optimization_barrier(slabs).astype(jnp.float32)
        blocked = inputs.reshape(RELATIONS + 1, N_FEAT, FEAT_IN // N_FEAT, DEST)
        partial_value = jnp.einsum("snfd,snfh->ndh", blocked, weights_one)
        partial_value = lax.optimization_barrier(partial_value.astype(jnp.bfloat16)).astype(jnp.float32)
        return jax.nn.relu(jnp.sum(partial_value, axis=0)).astype(jnp.bfloat16)

    hidden_one = lax.map(first_layer, (feats, nbr_one, rel_one))
    all_rows = hidden_one.reshape(N_BATCH * DEST, HIDDEN_SIZE)
    block_start = (jnp.arange(DEST, dtype=jnp.int32) // ROWS) * ROWS

    def second_layer(operands):
        own_rows, owners, within, relation_ids = operands
        row_index = (owners[:, :, 0] * DEST + block_start[:, None] + within).astype(jnp.int32)
        picked = jnp.take(all_rows, row_index, axis=0)
        slabs = relation_means(picked, relation_ids, own_rows, -1, 1, 1)
        inputs = lax.optimization_barrier(slabs).astype(jnp.float32)
        blocked = inputs.reshape(RELATIONS + 1, DEST, N_FEAT, HIDDEN_SIZE // N_FEAT)
        partial_value = jnp.einsum("sdnk,snkh->ndh", blocked, weights_two)
        partial_value = lax.optimization_barrier(partial_value.astype(jnp.bfloat16)).astype(jnp.float32)
        return jax.nn.relu(jnp.sum(partial_value, axis=0)).astype(jnp.bfloat16)

    return lax.map(second_layer, (hidden_one, owner_two, local_two, rel_two))
```

```python
import jax
import jax.numpy as jnp
from jax import lax
from jax.experimental import pallas as pl
from jax.experimental.pallas import tpu as pltpu
from jax.sharding import PartitionSpec as P

RELATIONS = 4
FANOUT_ONE = 15
FANOUT_TWO = 10
ROWS = 64
LANES = 128


def build_table(feats, table):
    def step(chunk, carry):
        at = pl.multiple_of(chunk * LANES, LANES)
        columns = feats[:, pl.ds(at, LANES)].astype(jnp.float32)
        gap = jnp.zeros((LANES // 2 - columns.shape[0], LANES), jnp.float32)
        table[pl.ds(at, LANES), :] = jnp.concatenate([columns, gap, columns, gap], axis=0).T
        return carry

    lax.fori_loop(0, table.shape[0] // LANES, step, 0, unroll=4)


def build_relations(rel, by_row):
    for chunk in range(by_row.shape[0] // LANES):
        ids = rel[:, chunk * LANES : (chunk + 1) * LANES].astype(jnp.float32)
        ids = jnp.concatenate([ids, jnp.full((1, LANES), 4.0, jnp.float32)], axis=0)
        by_row[chunk * LANES : (chunk + 1) * LANES, :] = ids.T


def eight_means(base, nbr, table, by_row, picked):
    tile = (8, LANES)
    half = (lax.broadcasted_iota(jnp.int32, tile, 1) // 64).astype(jnp.float32)
    ids = by_row[pl.ds(base, 8), :]
    for k in range(FANOUT_ONE):
        for i in range(8):
            picked[k * 8 + i : k * 8 + i + 1, :] = table[pl.ds(nbr[k, base + i], 1), :]
    zero = jnp.zeros(tile, jnp.float32)
    low, high, low_count, high_count = zero, zero, zero, zero
    for k in range(FANOUT_ONE):
        rows = picked[k * 8 : (k + 1) * 8, :]
        own = jnp.broadcast_to(ids[:, k : k + 1], tile)
        in_low, in_high = own == half, own == half + 2.0
        low = low + jnp.where(in_low, rows, 0.0)
        high = high + jnp.where(in_high, rows, 0.0)
        low_count = low_count + jnp.where(in_low, 1.0, 0.0)
        high_count = high_count + jnp.where(in_high, 1.0, 0.0)
    return low / jnp.maximum(low_count, 1.0), high / jnp.maximum(high_count, 1.0)


def aggregate_kernel(nbr, feats, rel, means, own, table, by_row, picked):
    build_table(feats, table)
    build_relations(rel, by_row)

    def step(group, carry):
        at = pl.multiple_of(group * 16, 16)
        pairs = [
            eight_means(at + u * 8, nbr, table, by_row, picked.at[u]) for u in range(2)
        ]
        for side in range(2):
            both = jnp.concatenate([pair[side] for pair in pairs], axis=0)
            means[pl.ds(at, 16), side * LANES : (side + 1) * LANES] = both.astype(jnp.bfloat16)
        return carry

    lax.fori_loop(0, means.shape[0] // 16, step, 0)
    own[...] = table[0 : own.shape[0], :].astype(jnp.bfloat16)


def aggregate(columns, neighbours, relation_ids):
    sources = columns.shape[1]
    dest = neighbours.shape[1]
    vmem = pl.BlockSpec(memory_space=pltpu.VMEM)
    return pl.pallas_call(
        aggregate_kernel,
        out_shape=(
            jax.ShapeDtypeStruct((dest, 2 * LANES), jnp.bfloat16),
            jax.ShapeDtypeStruct((dest, LANES), jnp.bfloat16),
        ),
        in_specs=[pl.BlockSpec(memory_space=pltpu.SMEM), vmem, vmem],
        out_specs=(vmem, vmem),
        scratch_shapes=[
            pltpu.VMEM((sources, LANES), jnp.float32),
            pltpu.VMEM((dest, 16), jnp.float32),
            pltpu.VMEM((2, FANOUT_ONE * 8, LANES), jnp.float32),
        ],
        compiler_params=pltpu.CompilerParams(vmem_limit_bytes=32 << 20),
        cost_estimate=pl.CostEstimate(flops=200_000_000, bytes_accessed=2_000_000, transcendentals=0),
        name="aggregate",
    )(neighbours, columns, relation_ids)


def spread_weights(w_one):
    slabs, depth, width = w_one.shape
    padded = jnp.pad(w_one, ((0, 0), (0, 64 - depth), (0, 0)))
    relation = padded[1:].reshape(RELATIONS * 64, width)
    own = jnp.pad(padded[0], ((0, 64), (0, 0)))
    return relation, own


def body(feats, nbr_one, rel_one, w_one, owner_two, local_two, rel_two, w_two):
    batch_size = lax.axis_size("batch")
    block = w_two.shape[1]
    piece = block // batch_size
    mine = lax.dynamic_slice_in_dim(w_two, lax.axis_index("batch") * piece, piece, 1)
    along = lax.all_gather(mine, "feat", axis=0)
    weights = lax.all_gather(along, "batch", axis=0)

    means, own = aggregate(feats[0], nbr_one[0], rel_one[0])
    relation_w, own_w = spread_weights(w_one)
    partial = jnp.dot(means, relation_w, preferred_element_type=jnp.float32) + jnp.dot(
        own, own_w, preferred_element_type=jnp.float32
    )
    hidden_one = jax.nn.relu(
        lax.psum_scatter(
            partial.astype(jnp.bfloat16), "feat", scatter_dimension=0, tiled=True
        ).astype(jnp.float32)
    ).astype(jnp.bfloat16)
    everyone = lax.all_gather(hidden_one, "batch", axis=0, tiled=True)

    offset = lax.axis_index("feat") * ROWS
    owners = lax.dynamic_slice_in_dim(owner_two[0, :, :, 0], offset, ROWS, 0)
    within = lax.dynamic_slice_in_dim(local_two[0], offset, ROWS, 0)
    ids = lax.dynamic_slice_in_dim(rel_two[0], offset, ROWS, 0)
    span = batch_size * ROWS
    keys = ids * span + owners * ROWS + within
    labels = jnp.arange(RELATIONS * span, dtype=jnp.int32)
    table = jnp.zeros((ROWS, RELATIONS * span), jnp.bfloat16)
    for slot in range(FANOUT_TWO):
        table = table + (keys[:, slot][:, None] == labels[None, :]).astype(jnp.bfloat16)
    table = table.reshape(ROWS, RELATIONS, span)
    counts = jnp.stack(
        [jnp.maximum(jnp.sum((ids == r).astype(jnp.int32), axis=1), 1) for r in range(RELATIONS)]
    ).astype(jnp.float32)
    summed = jnp.einsum("drc,ch->rdh", table, everyone, preferred_element_type=jnp.float32)
    means_two = (summed / counts[:, :, None]).astype(jnp.bfloat16)
    inputs = jnp.concatenate([hidden_one[None], means_two], axis=0)
    groups = inputs.reshape(RELATIONS + 1, ROWS, lax.axis_size("feat"), batch_size, piece)
    running = jnp.einsum("sdfbk,bfskh->dh", groups, weights, preferred_element_type=jnp.float32)
    return jax.nn.relu(running).astype(jnp.bfloat16)[None]


def solution(mesh):
    in_specs = (
        P("batch", "feat", None),
        P("batch", None, None),
        P("batch", None, None),
        P(None, "feat", None),
        P("batch", None, None, None),
        P("batch", None, None),
        P("batch", None, None),
        P(None, "feat", None),
    )
    out_specs = P("batch", "feat", None)
    return jax.shard_map(body, mesh=mesh, in_specs=in_specs, out_specs=out_specs, check_vma=False)
```

```python
import functools

import jax
import jax.numpy as jnp
from jax import lax
from jax.experimental import pallas as pl
from jax.experimental.pallas import tpu as pltpu
from jax.sharding import PartitionSpec as P

RELATIONS = 4
FANOUT_ONE = 15
FANOUT_TWO = 10
ROWS = 64
LANES = 128
WIDTH = 1024
HALF = WIDTH // 2
FEAT = 16
SIDE = 4
BATCHES = 32
BF16 = jnp.bfloat16
F32 = jnp.float32


class Links:
    def __init__(self, send_sems, recv_sems, anyone):
        self.send_sems, self.recv_sems, self.anyone = send_sems, recv_sems, anyone
        self.count = 0
        self.sent = []

    def _copy(self, index, src, dst, device):
        return pltpu.make_async_remote_copy(
            src_ref=src,
            dst_ref=dst,
            send_sem=self.send_sems.at[index],
            recv_sem=self.recv_sems.at[index],
            device_id=device,
            device_id_type=pl.DeviceIdType.MESH,
        )

    def send(self, ref, device, to=None):
        index = self.count
        self.count += 1
        copy = self._copy(index, ref, ref if to is None else to, device)
        copy.start()
        self.sent.append(copy)
        return index

    def arrive(self, index, ref):
        self._copy(index, ref, ref, self.anyone).wait_recv()

    def finish(self):
        for copy in self.sent:
            copy.wait_send()


def build_table(feats, table, first, last):
    def step(chunk, carry):
        at = pl.multiple_of(chunk * LANES, LANES)
        columns = feats[:, pl.ds(at, LANES)].astype(F32)
        gap = jnp.zeros((LANES // 2 - columns.shape[0], LANES), F32)
        table[pl.ds(at, LANES), :] = jnp.concatenate([columns, gap, columns, gap], axis=0).T
        return carry

    lax.fori_loop(first, last, step, 0, unroll=4)


def build_relations(rel, by_row):
    for chunk in range(by_row.shape[0] // LANES):
        ids = rel[:, chunk * LANES : (chunk + 1) * LANES].astype(F32)
        ids = jnp.concatenate([ids, jnp.full((1, LANES), 4.0, F32)], axis=0)
        by_row[chunk * LANES : (chunk + 1) * LANES, :] = ids.T


def eight_means(base, nbr, table, by_row, picked):
    tile = (8, LANES)
    half = (lax.broadcasted_iota(jnp.int32, tile, 1) // 64).astype(F32)
    ids = by_row[pl.ds(base, 8), :]
    for k in range(FANOUT_ONE):
        for i in range(8):
            picked[k * 8 + i : k * 8 + i + 1, :] = table[pl.ds(nbr[k, base + i], 1), :]
    zero = jnp.zeros(tile, F32)
    low, high, low_count, high_count = zero, zero, zero, zero
    for k in range(FANOUT_ONE):
        rows = picked[k * 8 : (k + 1) * 8, :]
        own = jnp.broadcast_to(ids[:, k : k + 1], tile)
        in_low, in_high = own == half, own == half + 2.0
        low = low + jnp.where(in_low, rows, 0.0)
        high = high + jnp.where(in_high, rows, 0.0)
        low_count = low_count + jnp.where(in_low, 1.0, 0.0)
        high_count = high_count + jnp.where(in_high, 1.0, 0.0)
    return low / jnp.maximum(low_count, 1.0), high / jnp.maximum(high_count, 1.0)


def gather_block(block, row, nbr, table, by_row, picked, slabs):
    def step(group, carry):
        at = pl.multiple_of(group * 16, 16)
        base = pl.multiple_of(block * ROWS + at, 16)
        pairs = [
            eight_means(base + u * 8, nbr, table, by_row, picked.at[u]) for u in range(2)
        ]
        for side in range(2):
            both = jnp.concatenate([pair[side] for pair in pairs], axis=0)
            slabs[pl.ds(row + at, 16), side * LANES : (side + 1) * LANES] = both.astype(BF16)
        return carry

    lax.fori_loop(0, ROWS // 16, step, 0)
    start = pl.multiple_of(block * ROWS, ROWS)
    slabs[row : row + ROWS, 2 * LANES :] = table[pl.ds(start, ROWS), :].astype(BF16)


def kernel(
    nbr,
    feats,
    rel,
    w_one,
    counts,
    scale,
    w_two,
    out,
    table,
    by_row,
    picked,
    slabs,
    weights,
    hidden,
    send_right,
    send_left,
    from_left,
    from_right,
    summed,
    result,
    send_sems,
    recv_sems,
    local_sem,
):
    z = lax.axis_index("feat")
    place = lax.axis_index("batch")
    core = lax.rem(place, 2)
    x = lax.rem(place // 2, SIDE)
    y = place // (2 * SIDE)
    u = x + core * (y - x)
    v = y + core * (x - y)

    def along(offset):
        return lax.rem(z + (FEAT + offset), FEAT)

    def turn(value, offset):
        return lax.rem(value + (SIDE + offset), SIDE)

    def in_plane(u_at, v_at):
        return (z, v_at * (8 - 6 * core) + u_at * (2 + 6 * core) + core)

    right, left = (along(1), place), (along(-1), place)
    u_next, u_prev = in_plane(turn(u, 1), v), in_plane(turn(u, -1), v)
    v_next, v_prev = in_plane(u, turn(v, 1)), in_plane(u, turn(v, -1))
    peer = (z, place + 1 - 2 * core)

    barrier = pltpu.get_barrier_semaphore()
    neighbours = (right, left, u_next, u_prev, v_next, v_prev, peer)
    for device in neighbours:
        pl.semaphore_signal(barrier, inc=1, device_id=device, device_id_type=pl.DeviceIdType.MESH)
    local = pltpu.make_async_copy(w_two, weights.at[:, z], local_sem)
    local.start()
    build_relations(rel, by_row)
    build_table(feats, table, 0, 16)
    local.wait()
    pl.semaphore_wait(barrier, len(neighbours))

    links = Links(send_sems, recv_sems, peer)

    def piece(f, u_at):
        return weights.at[:, f, v, :, pl.ds(pl.multiple_of((core * SIDE + u_at) * LANES, LANES), LANES)]

    def stripe(f, v_at):
        return weights.at[:, f, v_at, :, pl.ds(pl.multiple_of(core * HALF, HALF), HALF)]

    def column_half(f, which):
        return weights.at[:, f, :, :, pl.ds(pl.multiple_of(which * HALF, HALF), HALF)]

    z_sent, one, one_far, two, two_far, across = {}, {}, {}, {}, {}, {}

    def sides(t):
        return (-1, 1) if t < FEAT // 2 else (-1,)

    def z_step(t):
        for side in sides(t):
            device = right if side < 0 else left
            z_sent[t, side] = links.send(piece(along(side * (t - 1)), u), device)

    def z_arrive(t):
        for side in sides(t):
            links.arrive(z_sent[t, side], piece(along(side * t), u))

    def one_step(t):
        for side in sides(t):
            f = along(side * t)
            one[t, side] = (links.send(piece(f, u), u_next), links.send(piece(f, u), u_prev))

    def one_far_step(t):
        for side in sides(t):
            f = along(side * t)
            links.arrive(one[t, side][0], piece(f, turn(u, -1)))
            links.arrive(one[t, side][1], piece(f, turn(u, 1)))
            if side < 0:
                one_far[t, side] = links.send(piece(f, turn(u, -1)), u_next)
            else:
                one_far[t, side] = links.send(piece(f, turn(u, 1)), u_prev)

    def two_step(t):
        for side in sides(t):
            f = along(side * t)
            links.arrive(one_far[t, side], piece(f, turn(u, 2)))
            two[t, side] = (links.send(stripe(f, v), v_next), links.send(stripe(f, v), v_prev))

    def two_far_step(t):
        for side in sides(t):
            f = along(side * t)
            links.arrive(two[t, side][0], stripe(f, turn(v, -1)))
            links.arrive(two[t, side][1], stripe(f, turn(v, 1)))
            if side < 0:
                two_far[t, side] = links.send(stripe(f, turn(v, -1)), v_next)
            else:
                two_far[t, side] = links.send(stripe(f, turn(v, 1)), v_prev)

    def across_step(t):
        for side in sides(t):
            f = along(side * t)
            links.arrive(two_far[t, side], stripe(f, turn(v, 2)))
            across[t, side] = links.send(column_half(f, core), peer)

    steps = FEAT // 2

    def serve(slot):
        if 1 <= slot <= steps:
            z_arrive(slot)
            if slot < steps:
                z_step(slot + 1)
        for lag, action in enumerate((one_step, one_far_step, two_step, two_far_step, across_step)):
            t, odd = divmod(slot - lag, 2)
            if not odd and 1 <= t <= steps:
                action(t)

    z_step(1)
    for quarter in range(1, 4):
        build_table(feats, table, 16 * quarter, 16 * quarter + 16)
        serve(quarter)

    in_right, in_left = {}, {}
    slot = 4
    for s in range(steps + 1):
        gather_block(along(steps - s), 0, nbr, table, by_row, picked, slabs)
        serve(slot)
        slot += 1
        if 0 < s < steps:
            gather_block(along(s - steps), ROWS, nbr, table, by_row, picked, slabs)
        serve(slot)
        slot += 1
        rows = 2 * ROWS if 0 < s < steps else ROWS
        for h in range(2):
            columns = slice(h * HALF, (h + 1) * HALF)
            partial = jnp.dot(slabs[0:rows, :], w_one[:, columns], preferred_element_type=F32)
            if s == 0:
                if h == 0:
                    send_right[0, 0] = partial.astype(BF16)
                    in_right[0, 0] = links.send(send_right.at[0, 0], right, from_left.at[0, 0])
                else:
                    send_left[0, 1] = partial.astype(BF16)
                    in_left[0, 1] = links.send(send_left.at[0, 1], left, from_right.at[0, 1])
                continue
            if s == steps:
                links.arrive(in_right[s - 1, h], from_left.at[s - 1, h])
                links.arrive(in_left[s - 1, h], from_right.at[s - 1, h])
                total = partial + from_left[s - 1, h].astype(F32) + from_right[s - 1, h].astype(F32)
                hidden[core, v, u, :, columns] = jnp.maximum(total, 0.0).astype(BF16)
                continue
            onward, back = partial[:ROWS], partial[ROWS:]
            if (s - 1, h) in in_right:
                links.arrive(in_right[s - 1, h], from_left.at[s - 1, h])
                onward = onward + from_left[s - 1, h].astype(F32)
            send_right[s, h] = onward.astype(BF16)
            in_right[s, h] = links.send(send_right.at[s, h], right, from_left.at[s, h])
            if (s - 1, h) in in_left:
                links.arrive(in_left[s - 1, h], from_right.at[s - 1, h])
                back = back + from_right[s - 1, h].astype(F32)
            send_left[s, h] = back.astype(BF16)
            in_left[s, h] = links.send(send_left.at[s, h], left, from_right.at[s, h])

    def rows_of(du, dv, part=None):
        ref = hidden.at[core, turn(v, dv), turn(u, du)]
        if part is None:
            return ref
        return ref.at[pl.ds(part * (ROWS // 2), ROWS // 2)]

    def rows_of_peer(du, dv):
        return hidden.at[1 - core, turn(u, dv), turn(v, du)]

    u_direct = (links.send(rows_of(0, 0), u_next), links.send(rows_of(0, 0), u_prev))
    v_direct, v_far, crossed = {}, {}, {}

    def cross(du, dv):
        crossed[du, dv] = links.send(rows_of(du, dv), peer)

    def v_send(du):
        v_direct[du] = (links.send(rows_of(du, 0), v_next), links.send(rows_of(du, 0), v_prev))

    def v_forward(du):
        links.arrive(v_direct[du][0], rows_of(du, -1))
        links.arrive(v_direct[du][1], rows_of(du, 1))
        v_far[du] = (
            links.send(rows_of(du, -1, 0), v_next),
            links.send(rows_of(du, 1, 1), v_prev),
        )
        cross(du, -1)
        cross(du, 1)

    def v_arrive_far(du):
        links.arrive(v_far[du][0], rows_of(du, 2, 0))
        links.arrive(v_far[du][1], rows_of(du, 2, 1))
        cross(du, 2)

    def add_group(which, v_at, first=False):
        group = which * SIDE + v_at
        columns = pl.ds(pl.multiple_of(group * 2 * LANES, 2 * LANES), 2 * LANES)

        def step(n, carry):
            at = pl.ds(pl.multiple_of(n * 256, 256), 256)
            rows = hidden[which, v_at, :, :, at].reshape(SIDE * ROWS, 256)
            product = jnp.dot(counts[:, columns], rows, preferred_element_type=F32)
            summed[:, at] = product if first else summed[:, at] + product
            return carry

        lax.fori_loop(0, WIDTH // 256, step, 0)

    def times_weights(slab, left_rows, first=False):
        def step(n, carry):
            at = pl.ds(pl.multiple_of(n * 256, 256), 256)
            w = weights[slab, :, :, :, at].reshape(WIDTH, 256)
            product = jnp.dot(left_rows, w, preferred_element_type=F32)
            result[:, at] = product if first else result[:, at] + product
            return carry

        lax.fori_loop(0, WIDTH // 256, step, 0)

    v_send(0)
    cross(0, 0)
    links.arrive(u_direct[0], rows_of(-1, 0))
    links.arrive(u_direct[1], rows_of(1, 0))
    u_far = (links.send(rows_of(-1, 0, 0), u_next), links.send(rows_of(1, 0, 1), u_prev))
    v_send(-1)
    v_send(1)
    cross(-1, 0)
    cross(1, 0)
    v_forward(0)
    links.arrive(u_far[0], rows_of(2, 0, 0))
    links.arrive(u_far[1], rows_of(2, 0, 1))
    v_send(2)
    cross(2, 0)
    add_group(core, v, first=True)
    v_forward(-1)
    v_forward(1)
    v_arrive_far(0)
    for t in range(1, steps + 1):
        for side in sides(t):
            links.arrive(across[t, side], column_half(along(side * t), 1 - core))
    times_weights(0, hidden[core, v, u], first=True)
    for du in (0, -1, 1, 2):
        links.arrive(crossed[du, 0], rows_of_peer(du, 0))
    add_group(1 - core, u)
    v_forward(2)
    v_arrive_far(-1)
    v_arrive_far(1)
    for dv in (-1, 1):
        add_group(core, turn(v, dv))
    v_arrive_far(2)
    for dv in (-1, 1):
        for du in (0, -1, 1, 2):
            links.arrive(crossed[du, dv], rows_of_peer(du, dv))
        add_group(1 - core, turn(u, dv))
    add_group(core, turn(v, 2))
    for du in (0, -1, 1, 2):
        links.arrive(crossed[du, 2], rows_of_peer(du, 2))
    add_group(1 - core, turn(u, 2))

    for r in range(RELATIONS):
        mean = summed[r * ROWS : (r + 1) * ROWS, :] / scale[r * ROWS : (r + 1) * ROWS, :]
        times_weights(r + 1, mean.astype(BF16))
    out[...] = jnp.maximum(result[...], 0.0).astype(BF16)
    links.finish()


COPIES = 192


def two_layers(nbr, feats, rel, w_one, counts, scale, w_two):
    sources = feats.shape[1]
    dest = nbr.shape[1]
    vmem = pl.BlockSpec(memory_space=pltpu.VMEM)
    half_steps = FEAT // 2
    travelling = pltpu.VMEM((half_steps, 2, ROWS, HALF), BF16)
    return pl.pallas_call(
        kernel,
        out_shape=jax.ShapeDtypeStruct((ROWS, WIDTH), BF16),
        in_specs=[pl.BlockSpec(memory_space=pltpu.SMEM)]
        + [vmem] * 5
        + [pl.BlockSpec(memory_space=pl.ANY)],
        out_specs=vmem,
        scratch_shapes=[
            pltpu.VMEM((sources, LANES), F32),
            pltpu.VMEM((dest, 16), F32),
            pltpu.VMEM((2, FANOUT_ONE * 8, LANES), F32),
            pltpu.VMEM((2 * ROWS, 3 * LANES), BF16),
            pltpu.VMEM((RELATIONS + 1, FEAT, SIDE, ROWS // SIDE, WIDTH), BF16),
            pltpu.VMEM((2, SIDE, SIDE, ROWS, WIDTH), BF16),
            travelling,
            travelling,
            travelling,
            travelling,
            pltpu.VMEM((RELATIONS * ROWS, WIDTH), F32),
            pltpu.VMEM((ROWS, WIDTH), F32),
            pltpu.SemaphoreType.DMA((COPIES + 32,)),
            pltpu.SemaphoreType.DMA((COPIES + 32,)),
            pltpu.SemaphoreType.DMA,
        ],
        compiler_params=pltpu.CompilerParams(
            vmem_limit_bytes=48 << 20, collective_id=0, has_side_effects=True
        ),
        cost_estimate=pl.CostEstimate(
            flops=2_400_000_000, bytes_accessed=4_000_000, transcendentals=0
        ),
        name="two_layers",
    )(nbr, feats, rel, w_one, counts, scale, w_two)


def spread_weights(w_one):
    padded = jnp.pad(w_one, ((0, 0), (0, 64 - w_one.shape[1]), (0, 0)))
    relation = padded[1:].reshape(RELATIONS * 64, w_one.shape[2])
    return jnp.concatenate([relation, padded[0], jnp.zeros_like(padded[0])], axis=0)


def count_table(owner_two, local_two, rel_two):
    offset = lax.axis_index("feat") * ROWS
    owners = lax.dynamic_slice_in_dim(owner_two, offset, ROWS, 0)
    within = lax.dynamic_slice_in_dim(local_two, offset, ROWS, 0)
    ids = lax.dynamic_slice_in_dim(rel_two, offset, ROWS, 0)
    core, x, y = owners % 2, (owners // 2) % SIDE, owners // (2 * SIDE)
    held = jnp.where(core == 0, y * SIDE + x, SIDE * SIDE + x * SIDE + y)
    span = BATCHES * ROWS
    keys = ids * span + held * ROWS + within
    labels = jnp.arange(RELATIONS * span, dtype=jnp.int32)
    table = jnp.zeros((ROWS, RELATIONS * span), BF16)
    for slot in range(FANOUT_TWO):
        table = table + (keys[:, slot][:, None] == labels[None, :]).astype(BF16)
    table = table.reshape(ROWS, RELATIONS, span).transpose(1, 0, 2).reshape(RELATIONS * ROWS, span)
    counted = jnp.stack(
        [jnp.maximum(jnp.sum((ids == r).astype(jnp.int32), axis=1), 1) for r in range(RELATIONS)]
    ).astype(F32)
    return table, counted.reshape(RELATIONS * ROWS, 1)


def body(feats, nbr_one, rel_one, w_one, owner_two, local_two, rel_two, w_two):
    counts, scale = count_table(owner_two[0, :, :, 0], local_two[0], rel_two[0])
    pieces = w_two.reshape(RELATIONS + 1, SIDE, ROWS // SIDE, WIDTH)
    out = two_layers(nbr_one[0], feats[0], rel_one[0], spread_weights(w_one), counts, scale, pieces)
    return out[None]


def solution(mesh):
    in_specs = (
        P("batch", "feat", None),
        P("batch", None, None),
        P("batch", None, None),
        P(None, "feat", None),
        P("batch", None, None, None),
        P("batch", None, None),
        P("batch", None, None),
        P(None, "feat", None),
    )
    out_specs = P("batch", "feat", None)
    return jax.shard_map(body, mesh=mesh, in_specs=in_specs, out_specs=out_specs, check_vma=False)
```

```python
import jax
import jax.numpy as jnp
from jax import lax
from jax.experimental import pallas as pl
from jax.experimental.pallas import tpu as pltpu
from jax.sharding import PartitionSpec as P

RELATIONS = 4
FANOUT_ONE = 15
FANOUT_TWO = 10
ROWS = 64
LANES = 128
WIDTH = 1024
HALF = WIDTH // 2
FEAT = 16
SIDE = 4
BATCHES = 32
DEST_ROWS = 8
BF16 = jnp.bfloat16
F32 = jnp.float32


class Links:
    def __init__(self, send_sems, recv_sems, anyone):
        self.send_sems, self.recv_sems, self.anyone = send_sems, recv_sems, anyone
        self.count = 0
        self.sent = []

    def _copy(self, index, src, dst, device):
        return pltpu.make_async_remote_copy(
            src_ref=src,
            dst_ref=dst,
            send_sem=self.send_sems.at[index],
            recv_sem=self.recv_sems.at[index],
            device_id=device,
            device_id_type=pl.DeviceIdType.MESH,
        )

    def send(self, ref, device, to=None):
        index = self.count
        assert index < COPIES
        self.count += 1
        copy = self._copy(index, ref, ref if to is None else to, device)
        copy.start()
        self.sent.append(copy)
        return index

    def arrive(self, index, ref):
        self._copy(index, ref, ref, self.anyone).wait_recv()

    def finish(self):
        for copy in self.sent:
            copy.wait_send()


def build_table(feats, table, first, last):
    def step(chunk, carry):
        at = pl.multiple_of(chunk * LANES, LANES)
        columns = feats[:, pl.ds(at, LANES)].astype(F32)
        gap = jnp.zeros((LANES // 2 - columns.shape[0], LANES), F32)
        table[pl.ds(at, LANES), :] = jnp.concatenate([columns, gap, columns, gap], axis=0).T
        return carry

    lax.fori_loop(first, last, step, 0, unroll=4)


def as_columns(rows):
    rows = rows.astype(F32)
    left = jnp.full((16 - rows.shape[0], LANES), float(RELATIONS), F32)
    return jnp.concatenate([rows, left], axis=0).T


def build_relations(rel, by_row):
    for chunk in range(by_row.shape[0] // LANES):
        by_row[chunk * LANES : (chunk + 1) * LANES, :] = as_columns(rel[:, chunk, :])


def eight_means(base, row, column, nbr, table, by_row, picked):
    tile = (8, LANES)
    half = (lax.broadcasted_iota(jnp.int32, tile, 1) // 64).astype(F32)
    ids = by_row[pl.ds(base, 8), :]
    for k in range(FANOUT_ONE):
        for i in range(8):
            source = nbr[k, row, column + i]
            picked[k * 8 + i : k * 8 + i + 1, :] = table[pl.ds(source, 1), :]
    zero = jnp.zeros(tile, F32)
    low, high, low_count, high_count = zero, zero, zero, zero
    for k in range(FANOUT_ONE):
        rows = picked[k * 8 : (k + 1) * 8, :]
        own = jnp.broadcast_to(ids[:, k : k + 1], tile)
        in_low, in_high = own == half, own == half + 2.0
        low = low + jnp.where(in_low, rows, 0.0)
        high = high + jnp.where(in_high, rows, 0.0)
        low_count = low_count + jnp.where(in_low, 1.0, 0.0)
        high_count = high_count + jnp.where(in_high, 1.0, 0.0)
    return low / jnp.maximum(low_count, 1.0), high / jnp.maximum(high_count, 1.0)


def gather_block(block, to, nbr, table, by_row, picked, slabs):
    row, start = block // 2, lax.rem(block, 2) * ROWS

    def step(group, carry):
        at = pl.multiple_of(group * 16, 16)
        base = pl.multiple_of(block * ROWS + at, 16)
        pairs = [
            eight_means(base + n * 8, row, start + at + n * 8, nbr, table, by_row, picked.at[n])
            for n in range(2)
        ]
        for side in range(2):
            both = jnp.concatenate([pair[side] for pair in pairs], axis=0)
            slabs[pl.ds(to + at, 16), side * LANES : (side + 1) * LANES] = both.astype(BF16)
        return carry

    lax.fori_loop(0, ROWS // 16, step, 0)
    first = pl.multiple_of(block * ROWS, ROWS)
    slabs[to : to + ROWS, 2 * LANES :] = table[pl.ds(first, ROWS), :].astype(BF16)


def build_counts(keys, counts):
    span = counts.shape[1]

    def some_rows(n, carry):
        at = pl.multiple_of(n * 16, 16)
        key = keys[pl.ds(at, 16), :]
        spread = [jnp.broadcast_to(key[:, k : k + 1], (16, LANES)) for k in range(FANOUT_TWO)]
        lane = lax.broadcasted_iota(jnp.int32, (16, LANES), 1).astype(F32)
        for r in range(RELATIONS):
            for c in range(span // LANES):
                label = lane + float(r * span + c * LANES)
                total = jnp.zeros((16, LANES), F32)
                for k in range(FANOUT_TWO):
                    total = total + jnp.where(spread[k] == label, 1.0, 0.0)
                rows = pl.ds(r * ROWS + at, 16)
                counts[rows, c * LANES : (c + 1) * LANES] = total.astype(BF16)
        return carry

    lax.fori_loop(0, ROWS // 16, some_rows, 0)


def kernel(
    nbr_hbm,
    feats_hbm,
    rel_hbm,
    w_one_hbm,
    owner_hbm,
    within_hbm,
    ids_hbm,
    w_two,
    out,
    nbr,
    feats,
    rel,
    w_one,
    two,
    table,
    by_row,
    picked,
    slabs,
    keys,
    ids_two,
    counts,
    weights,
    hidden,
    send_right,
    send_left,
    from_left,
    from_right,
    summed,
    result,
    send_sems,
    recv_sems,
    local_sems,
):
    z = lax.axis_index("feat")
    place = lax.axis_index("batch")
    core = lax.rem(place, 2)
    x = lax.rem(place // 2, SIDE)
    y = place // (2 * SIDE)
    u = x + core * (y - x)
    v = y + core * (x - y)
    z_high, z_low = z // SIDE, lax.rem(z, SIDE)

    def along(offset):
        return lax.rem(z + (FEAT + offset), FEAT)

    def turn(value, offset):
        return lax.rem(value + (SIDE + offset), SIDE)

    def in_plane(u_at, v_at):
        return (z, v_at * (8 - 6 * core) + u_at * (2 + 6 * core) + core)

    z_by = {d: (along(d), place) for d in (1, -1, 2, -2, 4, -4, 8)}
    u_by = {d: in_plane(turn(u, d), v) for d in (1, -1, 2)}
    v_by = {d: in_plane(u, turn(v, d)) for d in (1, -1, 2)}
    right, left = z_by[1], z_by[-1]
    peer = (z, place + 1 - 2 * core)

    def own_columns(u_at):
        return pl.ds(pl.multiple_of((core * SIDE + u_at) * LANES, LANES), LANES)

    chunks = 4
    span = feats.shape[1] // chunks
    copies = [
        (feats_hbm.at[:, pl.ds(n * span, span)], feats.at[:, pl.ds(n * span, span)])
        for n in range(chunks)
    ] + [
        (w_two.at[:, v, :, own_columns(u)], weights.at[:, z_high, z_low, v, :, own_columns(u)]),
        (nbr_hbm, nbr),
        (rel_hbm, rel),
        (w_one_hbm.at[pl.ds(1, RELATIONS)], w_one.at[pl.ds(0, RELATIONS), pl.ds(0, 48)]),
        (w_one_hbm.at[pl.ds(0, 1)], w_one.at[pl.ds(RELATIONS, 1), pl.ds(0, 48)]),
        (owner_hbm, two.at[0]),
        (within_hbm, two.at[1]),
        (ids_hbm, two.at[2]),
    ]
    copies = [
        pltpu.make_async_copy(src, dst, local_sems.at[n]) for n, (src, dst) in enumerate(copies)
    ]
    for copy in copies:
        copy.start()

    barrier = pltpu.get_barrier_semaphore()
    neighbours = [*z_by.values(), *u_by.values(), *v_by.values(), peer]
    for device in neighbours:
        pl.semaphore_signal(barrier, inc=1, device_id=device, device_id_type=pl.DeviceIdType.MESH)

    links = Links(send_sems, recv_sems, peer)

    def piece(z_low_at, u_at, high=None):
        high = slice(None) if high is None else high
        return weights.at[:, high, z_low_at, v, :, own_columns(u_at)]

    def stripe(z_low_at, v_at, high=None):
        high = slice(None) if high is None else high
        return weights.at[
            :, high, z_low_at, v_at, :, pl.ds(pl.multiple_of(core * HALF, HALF), HALF)
        ]

    def column_half(z_low_at, which):
        return weights.at[:, :, z_low_at, :, :, pl.ds(pl.multiple_of(which * HALF, HALF), HALF)]

    first_half, last_half = pl.ds(0, SIDE // 2), pl.ds(SIDE // 2, SIDE // 2)
    sent = {}

    def z_far():
        copies[chunks].wait()
        for d in (4, -4, 8):
            sent["z", d] = links.send(piece(z_low, u, z_high), z_by[d])

    def z_near():
        for d in (4, -4, 8):
            links.arrive(sent["z", d], piece(z_low, u, along(-d) // SIDE))
        for d in (1, -1):
            sent["z", d] = links.send(piece(z_low, u), z_by[d])
        sent["z", 2] = links.send(piece(z_low, u, first_half), z_by[2])
        sent["z", -2] = links.send(piece(z_low, u, last_half), z_by[-2])

    def z_arrive(c):
        if c == 2:
            links.arrive(sent["z", 2], piece(turn(z_low, 2), u, first_half))
            links.arrive(sent["z", -2], piece(turn(z_low, 2), u, last_half))
        elif c:
            links.arrive(sent["z", -c], piece(turn(z_low, c), u))

    def u_step(c):
        z_arrive(c)
        for d in (1, -1):
            sent["u", c, d] = links.send(piece(turn(z_low, c), u), u_by[d])

    def u_far(c):
        at = turn(z_low, c)
        for d in (1, -1):
            links.arrive(sent["u", c, d], piece(at, turn(u, -d)))
        sent["u", c, 2] = links.send(piece(at, turn(u, -1), first_half), u_by[1])
        sent["u", c, -2] = links.send(piece(at, turn(u, 1), last_half), u_by[-1])

    def v_step(c):
        at = turn(z_low, c)
        links.arrive(sent["u", c, 2], piece(at, turn(u, 2), first_half))
        links.arrive(sent["u", c, -2], piece(at, turn(u, 2), last_half))
        for d in (1, -1):
            sent["v", c, d] = links.send(stripe(at, v), v_by[d])

    def v_far(c):
        at = turn(z_low, c)
        for d in (1, -1):
            links.arrive(sent["v", c, d], stripe(at, turn(v, -d)))
        sent["v", c, 2] = links.send(stripe(at, turn(v, -1), first_half), v_by[1])
        sent["v", c, -2] = links.send(stripe(at, turn(v, 1), last_half), v_by[-1])

    def across_step(c):
        at = turn(z_low, c)
        links.arrive(sent["v", c, 2], stripe(at, turn(v, 2), first_half))
        links.arrive(sent["v", c, -2], stripe(at, turn(v, 2), last_half))
        sent["across", c] = links.send(column_half(at, core), peer)

    plan = {
        2: [(z_near,), (u_step, 0)],
        4: [(u_far, 0), (u_step, 1), (u_step, -1)],
        6: [(u_step, 2), (v_step, 0), (u_far, 1), (u_far, -1)],
        8: [(v_step, 1), (v_step, -1), (u_far, 2)],
        9: [(v_far, 0)],
        10: [(v_step, 2)],
        12: [(across_step, 0), (v_far, 1)],
        14: [(v_far, -1), (across_step, 1)],
        16: [(v_far, 2), (across_step, -1)],
    }

    def serve(slot):
        for action, *given in plan.get(slot, ()):
            action(*given)

    for n in range(chunks):
        copies[n].wait()
        build_table(feats, table, n * span // LANES, (n + 1) * span // LANES)
        if n == 1:
            pl.semaphore_wait(barrier, len(neighbours))
            z_far()
    for copy in copies[chunks + 1 :]:
        copy.wait()
    build_relations(rel, by_row)
    w_one[:, 48:64, :] = jnp.zeros((6, 16, WIDTH), BF16)
    w_one[RELATIONS + 1, 0:48, :] = jnp.zeros((48, WIDTH), BF16)

    in_right, in_left = {}, {}
    steps = FEAT // 2
    quarter = WIDTH // 4
    for s in range(steps + 1):
        gather_block(along(steps - s), 0, nbr, table, by_row, picked, slabs)
        serve(2 * s)
        if 0 < s < steps:
            gather_block(along(s - steps), ROWS, nbr, table, by_row, picked, slabs)
        serve(2 * s + 1)
        rows = 2 * ROWS if 0 < s < steps else ROWS
        for h in range(4):
            columns = slice(h * quarter, (h + 1) * quarter)
            partial = jnp.dot(
                slabs[0:rows, :],
                w_one[:, :, columns].reshape(6 * 64, quarter),
                preferred_element_type=F32,
            )
            if s == 0:
                if h < 2:
                    send_right[0, h] = partial.astype(BF16)
                    in_right[0, h] = links.send(send_right.at[0, h], right, from_left.at[0, h])
                else:
                    send_left[0, h] = partial.astype(BF16)
                    in_left[0, h] = links.send(send_left.at[0, h], left, from_right.at[0, h])
                continue
            if s == steps:
                links.arrive(in_right[s - 1, h], from_left.at[s - 1, h])
                links.arrive(in_left[s - 1, h], from_right.at[s - 1, h])
                total = partial + from_left[s - 1, h].astype(F32) + from_right[s - 1, h].astype(F32)
                hidden[core, v, u, :, columns] = jnp.maximum(total, 0.0).astype(BF16)
                continue
            onward, back = partial[:ROWS], partial[ROWS:]
            if (s - 1, h) in in_right:
                links.arrive(in_right[s - 1, h], from_left.at[s - 1, h])
                onward = onward + from_left[s - 1, h].astype(F32)
            send_right[s, h] = onward.astype(BF16)
            in_right[s, h] = links.send(send_right.at[s, h], right, from_left.at[s, h])
            if (s - 1, h) in in_left:
                links.arrive(in_left[s - 1, h], from_right.at[s - 1, h])
                back = back + from_right[s - 1, h].astype(F32)
            send_left[s, h] = back.astype(BF16)
            in_left[s, h] = links.send(send_left.at[s, h], left, from_right.at[s, h])

    def rows_of(du, dv):
        return hidden.at[core, turn(v, dv), turn(u, du)]

    def rows_of_peer(du, dv):
        return hidden.at[1 - core, turn(u, dv), turn(v, du)]

    order = (0, -1, 1, 2)
    crossed = {}

    def cross(du, dv):
        crossed[du, dv] = links.send(rows_of(du, dv), peer)

    def to_v(du):
        for d in (1, -1, 2):
            sent["h", du, d] = links.send(rows_of(du, 0), v_by[d])

    def from_v(du, dv):
        links.arrive(sent["h", du, -dv if dv != 2 else 2], rows_of(du, dv))
        cross(du, dv)

    def add_group(which, v_at, first=False):
        group = which * SIDE + v_at
        columns = pl.ds(pl.multiple_of(group * 2 * LANES, 2 * LANES), 2 * LANES)

        def step(n, carry):
            at = pl.ds(pl.multiple_of(n * 256, 256), 256)
            rows = hidden[which, v_at, :, :, at].reshape(SIDE * ROWS, 256)
            product = jnp.dot(counts[:, columns], rows, preferred_element_type=F32)
            summed[:, at] = product if first else summed[:, at] + product
            return carry

        lax.fori_loop(0, WIDTH // 256, step, 0)

    def times_weights(slab, left_rows, first=False):
        def step(n, carry):
            at = pl.ds(pl.multiple_of(n * 256, 256), 256)
            w = weights[slab, :, :, :, :, at].reshape(WIDTH, 256)
            product = jnp.dot(left_rows, w, preferred_element_type=F32)
            result[:, at] = product if first else result[:, at] + product
            return carry

        lax.fori_loop(0, WIDTH // 256, step, 0)

    for d in (1, -1, 2):
        sent["hu", d] = links.send(rows_of(0, 0), u_by[d])
    to_v(0)
    cross(0, 0)

    block_row = z // 2
    owner, within, ids = (
        as_columns(two[n, :, pl.ds(block_row, 1), :].reshape(FANOUT_TWO, LANES)) for n in range(3)
    )
    owner = owner.astype(jnp.int32)
    parity, across_x, across_y = owner % 2, (owner // 2) % SIDE, owner // (2 * SIDE)
    held = across_y * SIDE + across_x + parity * (
        SIDE * SIDE + (SIDE - 1) * across_x - (SIDE - 1) * across_y
    )
    keys[...] = ids * float(BATCHES * ROWS) + held.astype(F32) * float(ROWS) + within
    ids_two[...] = ids
    mine = pl.ds(pl.multiple_of(lax.rem(z, 2) * ROWS, ROWS), ROWS)
    build_counts(keys.at[mine], counts)

    for du in (-1, 1, 2):
        links.arrive(sent["hu", -du if du != 2 else 2], rows_of(du, 0))
        to_v(du)
        cross(du, 0)
    add_group(core, v, first=True)
    for dv in (-1, 1, 2):
        from_v(0, dv)
    across_step(2)
    for c in (0, 1, -1, 2):
        links.arrive(sent["across", c], column_half(turn(z_low, c), 1 - core))
    times_weights(0, hidden[core, v, u], first=True)
    for du in order:
        links.arrive(crossed[du, 0], rows_of_peer(du, 0))
    add_group(1 - core, u)
    for dv in (-1, 1, 2):
        for du in (-1, 1, 2):
            from_v(du, dv)
        add_group(core, turn(v, dv))
    for dv in (-1, 1, 2):
        for du in order:
            links.arrive(crossed[du, dv], rows_of_peer(du, dv))
        add_group(1 - core, turn(u, dv))

    ids = ids_two[mine, :]
    for r in range(RELATIONS):
        number = jnp.sum(jnp.where(ids == float(r), 1.0, 0.0), axis=1, keepdims=True)
        mean = summed[r * ROWS : (r + 1) * ROWS, :] / jnp.maximum(number, 1.0)
        times_weights(r + 1, mean.astype(BF16))
    out[...] = jnp.maximum(result[...], 0.0).astype(BF16)
    links.finish()


COPIES = 144


def two_layers(nbr, feats, rel, w_one, owner, within, ids, w_two):
    sources = feats.shape[1]
    dest = WIDTH
    half_steps = FEAT // 2
    travelling = pltpu.VMEM((half_steps, 4, ROWS, WIDTH // 4), BF16)
    return pl.pallas_call(
        kernel,
        out_shape=jax.ShapeDtypeStruct((ROWS, WIDTH), BF16),
        in_specs=[pl.BlockSpec(memory_space=pl.ANY)] * 8,
        out_specs=pl.BlockSpec(memory_space=pltpu.VMEM),
        scratch_shapes=[
            pltpu.SMEM(nbr.shape, jnp.int32),
            pltpu.VMEM(feats.shape, BF16),
            pltpu.VMEM(rel.shape, jnp.int32),
            pltpu.VMEM((RELATIONS + 2, 64, WIDTH), BF16),
            pltpu.VMEM((3, *ids.shape), jnp.int32),
            pltpu.VMEM((sources, LANES), F32),
            pltpu.VMEM((dest, 16), F32),
            pltpu.VMEM((2, FANOUT_ONE * 8, LANES), F32),
            pltpu.VMEM((2 * ROWS, 3 * LANES), BF16),
            pltpu.VMEM((LANES, 16), F32),
            pltpu.VMEM((LANES, 16), F32),
            pltpu.VMEM((RELATIONS * ROWS, BATCHES * ROWS), BF16),
            pltpu.VMEM((RELATIONS + 1, SIDE, SIDE, SIDE, ROWS // SIDE, WIDTH), BF16),
            pltpu.VMEM((2, SIDE, SIDE, ROWS, WIDTH), BF16),
            travelling,
            travelling,
            travelling,
            travelling,
            pltpu.VMEM((RELATIONS * ROWS, WIDTH), F32),
            pltpu.VMEM((ROWS, WIDTH), F32),
            pltpu.SemaphoreType.DMA((COPIES,)),
            pltpu.SemaphoreType.DMA((COPIES,)),
            pltpu.SemaphoreType.DMA((12,)),
        ],
        compiler_params=pltpu.CompilerParams(
            vmem_limit_bytes=48 << 20, collective_id=0, has_side_effects=True
        ),
        cost_estimate=pl.CostEstimate(
            flops=2_400_000_000, bytes_accessed=4_000_000, transcendentals=0
        ),
        name="two_layers",
    )(nbr, feats, rel, w_one, owner, within, ids, w_two)


def body(feats, nbr_one, rel_one, w_one, owner_two, local_two, rel_two, w_two):
    def slots_first(array):
        return array.T.reshape(FANOUT_TWO, DEST_ROWS, LANES)

    out = two_layers(
        nbr_one[0].reshape(FANOUT_ONE, DEST_ROWS, LANES),
        feats[0],
        rel_one[0].reshape(FANOUT_ONE, DEST_ROWS, LANES),
        w_one,
        slots_first(owner_two[0, :, :, 0]),
        slots_first(local_two[0]),
        slots_first(rel_two[0]),
        w_two.reshape(RELATIONS + 1, SIDE, ROWS // SIDE, WIDTH),
    )
    return out[None]


def solution(mesh):
    in_specs = (
        P("batch", "feat", None),
        P("batch", None, None),
        P("batch", None, None),
        P(None, "feat", None),
        P("batch", None, None, None),
        P("batch", None, None),
        P("batch", None, None),
        P(None, "feat", None),
    )
    out_specs = P("batch", "feat", None)
    return jax.shard_map(body, mesh=mesh, in_specs=in_specs, out_specs=out_specs, check_vma=False)
```

```python
import jax
import jax.numpy as jnp
from jax import lax
from jax.experimental import pallas as pl
from jax.experimental.pallas import tpu as pltpu
from jax.sharding import PartitionSpec as P

RELATIONS = 4
FANOUT_ONE = 15
FANOUT_TWO = 10
ROWS = 64
LANES = 128
WIDTH = 1024
HALF = WIDTH // 2
FEAT = 16
SIDE = 4
BATCHES = 32
DEST_ROWS = 8
BF16 = jnp.bfloat16
F32 = jnp.float32


class Links:
    def __init__(self, send_sems, recv_sems, anyone):
        self.send_sems, self.recv_sems, self.anyone = send_sems, recv_sems, anyone
        self.count = 0
        self.sent = []

    def _copy(self, index, src, dst, device):
        return pltpu.make_async_remote_copy(
            src_ref=src,
            dst_ref=dst,
            send_sem=self.send_sems.at[index],
            recv_sem=self.recv_sems.at[index],
            device_id=device,
            device_id_type=pl.DeviceIdType.MESH,
        )

    def send(self, ref, device, to=None):
        index = self.count
        assert index < COPIES
        self.count += 1
        copy = self._copy(index, ref, ref if to is None else to, device)
        copy.start()
        self.sent.append(copy)
        return index

    def arrive(self, index, ref):
        self._copy(index, ref, ref, self.anyone).wait_recv()

    def finish(self):
        for copy in self.sent:
            copy.wait_send()


def build_table(feats, table, first, last):
    def step(chunk, carry):
        at = pl.multiple_of(chunk * LANES, LANES)
        columns = feats[:, pl.ds(at, LANES)].astype(F32)
        gap = jnp.zeros((LANES // 2 - columns.shape[0], LANES), F32)
        table[pl.ds(at, LANES), :] = jnp.concatenate([columns, gap, columns, gap], axis=0).T
        return carry

    lax.fori_loop(first, last, step, 0, unroll=4)


def as_columns(rows):
    rows = rows.astype(F32)
    left = jnp.full((16 - rows.shape[0], LANES), float(RELATIONS), F32)
    return jnp.concatenate([rows, left], axis=0).T


def build_relations(rel, by_row):
    for chunk in range(by_row.shape[0] // LANES):
        by_row[chunk * LANES : (chunk + 1) * LANES, :] = as_columns(rel[:, chunk, :])


def eight_means(base, row, column, nbr, table, by_row, picked):
    tile = (8, LANES)
    half = (lax.broadcasted_iota(jnp.int32, tile, 1) // 64).astype(F32)
    ids = by_row[pl.ds(base, 8), :]
    for k in range(FANOUT_ONE):
        for i in range(8):
            source = nbr[k, row, column + i]
            picked[k * 8 + i : k * 8 + i + 1, :] = table[pl.ds(source, 1), :]
    zero = jnp.zeros(tile, F32)
    low, high, low_count, high_count = zero, zero, zero, zero
    for k in range(FANOUT_ONE):
        rows = picked[k * 8 : (k + 1) * 8, :]
        own = jnp.broadcast_to(ids[:, k : k + 1], tile)
        in_low, in_high = own == half, own == half + 2.0
        low = low + jnp.where(in_low, rows, 0.0)
        high = high + jnp.where(in_high, rows, 0.0)
        low_count = low_count + jnp.where(in_low, 1.0, 0.0)
        high_count = high_count + jnp.where(in_high, 1.0, 0.0)
    return low / jnp.maximum(low_count, 1.0), high / jnp.maximum(high_count, 1.0)


def gather_block(block, to, nbr, table, by_row, picked, slabs):
    row, start = block // 2, lax.rem(block, 2) * ROWS

    def step(group, carry):
        at = pl.multiple_of(group * 16, 16)
        base = pl.multiple_of(block * ROWS + at, 16)
        pairs = [
            eight_means(base + n * 8, row, start + at + n * 8, nbr, table, by_row, picked.at[n])
            for n in range(2)
        ]
        for side in range(2):
            both = jnp.concatenate([pair[side] for pair in pairs], axis=0)
            slabs[pl.ds(to + at, 16), side * LANES : (side + 1) * LANES] = both.astype(BF16)
        return carry

    lax.fori_loop(0, ROWS // 16, step, 0)
    first = pl.multiple_of(block * ROWS, ROWS)
    slabs[to : to + ROWS, 2 * LANES :] = table[pl.ds(first, ROWS), :].astype(BF16)


def build_counts(keys, counts, first_row):
    span = counts.shape[1]

    def some_rows(n, carry):
        at = pl.multiple_of(n * 16, 16)
        key = keys[pl.ds(at, 16), :]
        tiles = jnp.floor(key * (1.0 / LANES))
        lane = lax.broadcasted_iota(jnp.int32, (16, LANES), 1).astype(F32)
        tile_of, ones = [], []
        for k in range(FANOUT_TWO):
            column = jnp.broadcast_to(key[:, k : k + 1], (16, LANES))
            tile = jnp.broadcast_to(tiles[:, k : k + 1], (16, LANES))
            tile_of.append(tile.astype(BF16))
            ones.append(jnp.where(column - tile * LANES == lane, 1.0, 0.0).astype(BF16))
        zero = jnp.zeros((16, LANES), BF16)
        for r in range(RELATIONS):
            for c in range(span // LANES):
                label = jnp.full((16, LANES), r * (span // LANES) + c, BF16)
                parts = [
                    jnp.where(tile_of[k] == label, ones[k], zero) for k in range(FANOUT_TWO)
                ]
                while len(parts) > 1:
                    parts = [sum(parts[i : i + 2][1:], parts[i]) for i in range(0, len(parts), 2)]
                rows = pl.ds(r * SIDE * ROWS + first_row + at, 16)
                counts[rows, c * LANES : (c + 1) * LANES] = parts[0]
        return carry

    lax.fori_loop(0, ROWS // 16, some_rows, 0)


def kernel(
    nbr_hbm,
    feats_hbm,
    rel_hbm,
    w_one_hbm,
    owner_hbm,
    within_hbm,
    ids_hbm,
    w_two,
    out,
    nbr,
    feats,
    rel,
    w_one,
    two,
    table,
    by_row,
    picked,
    slabs,
    columns_two,
    keys,
    counts,
    weights,
    hidden,
    send_right,
    send_left,
    from_left,
    from_right,
    summed,
    left_rows,
    finished,
    arrived,
    send_sems,
    recv_sems,
    local_sems,
):
    z = lax.axis_index("feat")
    place = lax.axis_index("batch")
    core = lax.rem(place, 2)
    x = lax.rem(place // 2, SIDE)
    y = place // (2 * SIDE)
    u = x + core * (y - x)
    v = y + core * (x - y)
    z_high, z_low = z // SIDE, lax.rem(z, SIDE)

    def along(offset):
        return lax.rem(z + (FEAT + offset), FEAT)

    def turn(value, offset):
        return lax.rem(value + (SIDE + offset), SIDE)

    def in_plane(u_at, v_at):
        return (z, v_at * (8 - 6 * core) + u_at * (2 + 6 * core) + core)

    z_by = {d: (along(d), place) for d in (1, -1, 2, -2, 4, -4, 8)}
    u_by = {d: in_plane(turn(u, d), v) for d in (1, -1, 2)}
    v_by = {d: in_plane(u, turn(v, d)) for d in (1, -1, 2)}
    x_by = {d: (z, y * 2 * SIDE + turn(x, d) * 2 + core) for d in (1, -1, 2)}
    y_by = {d: (z, turn(y, d) * 2 * SIDE + x * 2 + core) for d in (1, -1, 2)}
    right, left = z_by[1], z_by[-1]
    peer = (z, place + 1 - 2 * core)

    wide = WIDTH // SIDE

    def lanes_of(which):
        return pl.ds(pl.multiple_of(which * LANES, LANES), LANES)

    here = pl.ds(pl.multiple_of(x * wide + core * LANES, LANES), LANES)

    chunks = 4
    span = feats.shape[1] // chunks
    copies = [
        (feats_hbm.at[:, pl.ds(n * span, span)], feats.at[:, pl.ds(n * span, span)])
        for n in range(chunks)
    ] + [
        (w_two.at[:, y, :, here], weights.at[:, z_high, z_low, y, :, lanes_of(core)]),
        (nbr_hbm, nbr),
        (rel_hbm, rel),
        (w_one_hbm.at[pl.ds(1, RELATIONS)], w_one.at[pl.ds(0, RELATIONS), pl.ds(0, 48)]),
        (w_one_hbm.at[pl.ds(0, 1)], w_one.at[pl.ds(RELATIONS, 1), pl.ds(0, 48)]),
        (owner_hbm, two.at[0]),
        (within_hbm, two.at[1]),
        (ids_hbm, two.at[2]),
    ]
    copies = [
        pltpu.make_async_copy(src, dst, local_sems.at[n]) for n, (src, dst) in enumerate(copies)
    ]
    for copy in copies:
        copy.start()

    barrier = pltpu.get_barrier_semaphore()
    neighbours = [*z_by.values(), *u_by.values(), *v_by.values(), peer]
    for device in neighbours:
        pl.semaphore_signal(barrier, inc=1, device_id=device, device_id_type=pl.DeviceIdType.MESH)

    links = Links(send_sems, recv_sems, peer)

    def piece(z_low_at, y_at, high=None):
        high = slice(None) if high is None else high
        return weights.at[:, high, z_low_at, y_at, :, lanes_of(core)]

    def column_half(z_low_at, which):
        return weights.at[:, :, z_low_at, :, :, lanes_of(which)]

    first_half, last_half = pl.ds(0, SIDE // 2), pl.ds(SIDE // 2, SIDE // 2)
    sent = {}

    def z_far():
        copies[chunks].wait()
        for d in (4, -4, 8):
            sent["z", d] = links.send(piece(z_low, y, z_high), z_by[d])

    def z_near():
        for d in (4, -4, 8):
            links.arrive(sent["z", d], piece(z_low, y, along(-d) // SIDE))
        for d in (1, -1):
            sent["z", d] = links.send(piece(z_low, y), z_by[d])
        sent["z", 2] = links.send(piece(z_low, y, first_half), z_by[2])
        sent["z", -2] = links.send(piece(z_low, y, last_half), z_by[-2])

    def z_arrive(c):
        if c == 2:
            links.arrive(sent["z", 2], piece(turn(z_low, 2), y, first_half))
            links.arrive(sent["z", -2], piece(turn(z_low, 2), y, last_half))
        elif c:
            links.arrive(sent["z", -c], piece(turn(z_low, c), y))

    def y_step(c):
        z_arrive(c)
        for d in (1, -1):
            sent["y", c, d] = links.send(piece(turn(z_low, c), y), y_by[d])

    def y_far(c):
        at = turn(z_low, c)
        for d in (1, -1):
            links.arrive(sent["y", c, d], piece(at, turn(y, -d)))
        sent["y", c, 2] = links.send(piece(at, turn(y, -1), first_half), y_by[1])
        sent["y", c, -2] = links.send(piece(at, turn(y, 1), last_half), y_by[-1])

    def across_step(c):
        at = turn(z_low, c)
        links.arrive(sent["y", c, 2], piece(at, turn(y, 2), first_half))
        links.arrive(sent["y", c, -2], piece(at, turn(y, 2), last_half))
        sent["across", c] = links.send(column_half(at, core), peer)

    plan = {
        3: [(z_near,), (y_step, 0)],
        6: [(y_far, 0)],
        7: [(y_step, 1), (y_step, -1)],
        8: [(y_step, 2)],
        10: [(across_step, 0), (y_far, 1)],
        11: [(y_far, -1)],
        12: [(y_far, 2)],
        14: [(across_step, 1)],
        15: [(across_step, -1)],
        16: [(across_step, 2)],
    }

    def serve(slot):
        for action, *given in plan.get(slot, ()):
            action(*given)

    for n in range(chunks):
        copies[n].wait()
        build_table(feats, table, n * span // LANES, (n + 1) * span // LANES)
        if n == 1:
            pl.semaphore_wait(barrier, len(neighbours))
            z_far()
    for copy in copies[chunks + 1 :]:
        copy.wait()
    build_relations(rel, by_row)
    block_row = z // 2
    owner, within, ids = (
        as_columns(two[n, :, pl.ds(block_row, 1), :].reshape(FANOUT_TWO, LANES)) for n in range(3)
    )
    owner = owner.astype(jnp.int32)
    parity, across_x, across_y = owner % 2, (owner // 2) % SIDE, owner // (2 * SIDE)
    held = across_y * SIDE + across_x + parity * (
        SIDE * SIDE + (SIDE - 1) * across_x - (SIDE - 1) * across_y
    )
    columns_two[...] = ids * float(BATCHES * ROWS) + held.astype(F32) * float(ROWS) + within
    mine = pl.ds(pl.multiple_of(lax.rem(z, 2) * ROWS, ROWS), ROWS)
    none = jnp.full((ROWS, LANES - 16), float(RELATIONS * BATCHES * ROWS), F32)
    keys[x] = jnp.concatenate([columns_two[mine, :], none], axis=1)
    for d in (1, -1, 2):
        sent["keys", d] = links.send(keys.at[x], x_by[d])
    w_one[:, 48:64, :] = jnp.zeros((6, 16, WIDTH), BF16)
    w_one[RELATIONS + 1, 0:48, :] = jnp.zeros((48, WIDTH), BF16)

    in_right, in_left = {}, {}
    steps = FEAT // 2
    quarter = WIDTH // 4
    for s in range(steps + 1):
        gather_block(along(steps - s), 0, nbr, table, by_row, picked, slabs)
        serve(2 * s)
        if 0 < s < steps:
            gather_block(along(s - steps), ROWS, nbr, table, by_row, picked, slabs)
        serve(2 * s + 1)
        rows = 2 * ROWS if 0 < s < steps else ROWS
        for h in range(4):
            columns = slice(h * quarter, (h + 1) * quarter)
            partial = jnp.dot(
                slabs[0:rows, :],
                w_one[:, :, columns].reshape(6 * 64, quarter),
                preferred_element_type=F32,
            )
            if s == 0:
                if h < 2:
                    send_right[0, h] = partial.astype(BF16)
                    in_right[0, h] = links.send(send_right.at[0, h], right, from_left.at[0, h])
                else:
                    send_left[0, h] = partial.astype(BF16)
                    in_left[0, h] = links.send(send_left.at[0, h], left, from_right.at[0, h])
                continue
            if s == steps:
                links.arrive(in_right[s - 1, h], from_left.at[s - 1, h])
                links.arrive(in_left[s - 1, h], from_right.at[s - 1, h])
                total = partial + from_left[s - 1, h].astype(F32) + from_right[s - 1, h].astype(F32)
                hidden[core, v, u, :, columns] = jnp.maximum(total, 0.0).astype(BF16)
                continue
            onward, back = partial[:ROWS], partial[ROWS:]
            if (s - 1, h) in in_right:
                links.arrive(in_right[s - 1, h], from_left.at[s - 1, h])
                onward = onward + from_left[s - 1, h].astype(F32)
            send_right[s, h] = onward.astype(BF16)
            in_right[s, h] = links.send(send_right.at[s, h], right, from_left.at[s, h])
            if (s - 1, h) in in_left:
                links.arrive(in_left[s - 1, h], from_right.at[s - 1, h])
                back = back + from_right[s - 1, h].astype(F32)
            send_left[s, h] = back.astype(BF16)
            in_left[s, h] = links.send(send_left.at[s, h], left, from_right.at[s, h])

    def rows_of(du, dv):
        return hidden.at[core, turn(v, dv), turn(u, du)]

    def rows_of_peer(du, dv):
        return hidden.at[1 - core, turn(u, dv), turn(v, du)]

    order = (0, -1, 1, 2)
    crossed = {}

    def cross(du, dv):
        crossed[du, dv] = links.send(rows_of(du, dv), peer)

    def to_v(du):
        for d in (1, -1, 2) if du == 2 else (1, -1):
            sent["h", du, d] = links.send(rows_of(du, 0), v_by[d])

    def half_of(ref, which):
        return ref.at[pl.ds(which * (ROWS // 2), ROWS // 2)]

    def from_v(du):
        for d in (1, -1):
            links.arrive(sent["h", du, d], rows_of(du, -d))
        if du != 2:
            sent["h", du, 2] = links.send(half_of(rows_of(du, -1), 0), v_by[1])
            sent["h", du, -2] = links.send(half_of(rows_of(du, 1), 1), v_by[-1])
        cross(du, -1)
        cross(du, 1)

    def from_v_far(du):
        if du == 2:
            links.arrive(sent["h", du, 2], rows_of(du, 2))
        else:
            links.arrive(sent["h", du, 2], half_of(rows_of(du, 2), 0))
            links.arrive(sent["h", du, -2], half_of(rows_of(du, 2), 1))
        cross(du, 2)

    def add_group(which, v_at, first=False):
        group = which * SIDE + v_at
        columns = pl.ds(pl.multiple_of(group * 2 * LANES, 2 * LANES), 2 * LANES)

        def step(n, carry):
            at = pl.ds(pl.multiple_of(n * 256, 256), 256)
            rows = hidden[which, v_at, :, :, at].reshape(SIDE * ROWS, 256)
            for r in range(RELATIONS):
                some = slice(r * SIDE * ROWS, (r + 1) * SIDE * ROWS)
                product = jnp.dot(counts[some, columns], rows, preferred_element_type=F32)
                summed[some, at] = product if first else summed[some, at] + product
            return carry

        lax.fori_loop(0, WIDTH // 256, step, 0)

    for d in (1, -1, 2):
        sent["hu", d] = links.send(rows_of(0, 0), u_by[d])
    to_v(0)
    cross(0, 0)

    def count(d):
        if d:
            links.arrive(sent["keys", d], keys.at[turn(x, -d)])
        build_counts(keys.at[turn(x, -d)], counts, turn(x, -d) * ROWS)

    count(0)
    count(1)
    for du in (-1, 1, 2):
        links.arrive(sent["hu", -du if du != 2 else 2], rows_of(du, 0))
        to_v(du)
        cross(du, 0)
    count(-1)
    from_v(0)
    count(2)
    add_group(core, v, first=True)
    for du in (-1, 1):
        from_v(du)
    for du in order:
        links.arrive(crossed[du, 0], rows_of_peer(du, 0))
    add_group(1 - core, u)
    from_v_far(0)
    from_v(2)
    add_group(core, turn(v, -1))
    from_v_far(2)
    from_v_far(-1)
    from_v_far(1)
    add_group(core, turn(v, 1))
    add_group(core, turn(v, 2))
    for dv in (-1, 1, 2):
        for du in order:
            links.arrive(crossed[du, dv], rows_of_peer(du, dv))
        add_group(1 - core, turn(u, dv))
    for c in (0, 1, -1, 2):
        links.arrive(sent["across", c], column_half(turn(z_low, c), 1 - core))

    ring_rows = SIDE * ROWS
    for n in range(SIDE):
        own = hidden[core, y + core * (n - y), n + core * (y - n)]
        left_rows[0, n * ROWS : (n + 1) * ROWS, :] = own
        key = keys[n]
        for r in range(RELATIONS):
            low, high = float(r * BATCHES * ROWS), float((r + 1) * BATCHES * ROWS)
            inside = jnp.where((key >= low) & (key < high), 1.0, 0.0)
            number = jnp.maximum(jnp.sum(inside, axis=1, keepdims=True), 1.0)
            some = slice(r * ring_rows + n * ROWS, r * ring_rows + (n + 1) * ROWS)
            left_rows[r + 1, n * ROWS : (n + 1) * ROWS, :] = (summed[some, :] / number).astype(BF16)
    total = jnp.zeros((ring_rows, wide), F32)
    for slab in range(RELATIONS + 1):
        w = weights[slab].reshape(WIDTH, wide)
        total = total + jnp.dot(left_rows[slab], w, preferred_element_type=F32)
    finished[...] = jnp.maximum(total, 0.0).astype(BF16).reshape(SIDE, ROWS, wide)
    for d in (1, -1, 2):
        sent["out", d] = links.send(finished.at[turn(x, d)], x_by[d], arrived.at[x])
    arrived[x] = finished[x]
    for d in (1, -1, 2):
        links.arrive(sent["out", d], arrived.at[turn(x, -d)])
    for n in range(SIDE):
        out[:, n * wide : (n + 1) * wide] = arrived[n]
    links.finish()


COPIES = 144


def two_layers(nbr, feats, rel, w_one, owner, within, ids, w_two):
    sources = feats.shape[1]
    dest = WIDTH
    half_steps = FEAT // 2
    travelling = pltpu.VMEM((half_steps, 4, ROWS, WIDTH // 4), BF16)
    return pl.pallas_call(
        kernel,
        out_shape=jax.ShapeDtypeStruct((ROWS, WIDTH), BF16),
        in_specs=[pl.BlockSpec(memory_space=pl.ANY)] * 8,
        out_specs=pl.BlockSpec(memory_space=pltpu.VMEM),
        scratch_shapes=[
            pltpu.SMEM(nbr.shape, jnp.int32),
            pltpu.VMEM(feats.shape, BF16),
            pltpu.VMEM(rel.shape, jnp.int32),
            pltpu.VMEM((RELATIONS + 2, 64, WIDTH), BF16),
            pltpu.VMEM((3, *ids.shape), jnp.int32),
            pltpu.VMEM((sources, LANES), F32),
            pltpu.VMEM((dest, 16), F32),
            pltpu.VMEM((2, FANOUT_ONE * 8, LANES), F32),
            pltpu.VMEM((2 * ROWS, 3 * LANES), BF16),
            pltpu.VMEM((LANES, 16), F32),
            pltpu.VMEM((SIDE, ROWS, LANES), F32),
            pltpu.VMEM((RELATIONS * SIDE * ROWS, BATCHES * ROWS), BF16),
            pltpu.VMEM((RELATIONS + 1, SIDE, SIDE, SIDE, ROWS // SIDE, WIDTH // SIDE), BF16),
            pltpu.VMEM((2, SIDE, SIDE, ROWS, WIDTH), BF16),
            travelling,
            travelling,
            travelling,
            travelling,
            pltpu.VMEM((RELATIONS * SIDE * ROWS, WIDTH), F32),
            pltpu.VMEM((RELATIONS + 1, SIDE * ROWS, WIDTH), BF16),
            pltpu.VMEM((SIDE, ROWS, WIDTH // SIDE), BF16),
            pltpu.VMEM((SIDE, ROWS, WIDTH // SIDE), BF16),
            pltpu.SemaphoreType.DMA((COPIES,)),
            pltpu.SemaphoreType.DMA((COPIES,)),
            pltpu.SemaphoreType.DMA((12,)),
        ],
        compiler_params=pltpu.CompilerParams(
            vmem_limit_bytes=62 << 20, collective_id=0, has_side_effects=True
        ),
        cost_estimate=pl.CostEstimate(
            flops=2_400_000_000, bytes_accessed=4_000_000, transcendentals=0
        ),
        name="two_layers",
    )(nbr, feats, rel, w_one, owner, within, ids, w_two)


def body(feats, nbr_one, rel_one, w_one, owner_two, local_two, rel_two, w_two):
    def slots_first(array):
        return array.reshape(DEST_ROWS, LANES, FANOUT_TWO).transpose(2, 0, 1)

    out = two_layers(
        nbr_one[0].reshape(FANOUT_ONE, DEST_ROWS, LANES),
        feats[0],
        rel_one[0].reshape(FANOUT_ONE, DEST_ROWS, LANES),
        w_one,
        slots_first(owner_two[0, :, :, 0]),
        slots_first(local_two[0]),
        slots_first(rel_two[0]),
        w_two.reshape(RELATIONS + 1, SIDE, ROWS // SIDE, WIDTH),
    )
    return out[None]


def solution(mesh):
    in_specs = (
        P("batch", "feat", None),
        P("batch", None, None),
        P("batch", None, None),
        P(None, "feat", None),
        P("batch", None, None, None),
        P("batch", None, None),
        P("batch", None, None),
        P(None, "feat", None),
    )
    out_specs = P("batch", "feat", None)
    return jax.shard_map(body, mesh=mesh, in_specs=in_specs, out_specs=out_specs, check_vma=False)
```

```python
import jax
import jax.numpy as jnp
from jax import lax
from jax.experimental import pallas as pl
from jax.experimental.pallas import tpu as pltpu
from jax.sharding import PartitionSpec as P

RELATIONS = 4
FANOUT_ONE = 15
FANOUT_TWO = 10
ROWS = 64
LANES = 128
WIDTH = 1024
HALF = WIDTH // 2
FEAT = 16
SIDE = 4
BATCHES = 32
DEST_ROWS = 8
BF16 = jnp.bfloat16
F32 = jnp.float32


class Links:
    def __init__(self, send_sems, recv_sems, anyone):
        self.send_sems, self.recv_sems, self.anyone = send_sems, recv_sems, anyone
        self.count = 0
        self.sent = []

    def _copy(self, index, src, dst, device):
        return pltpu.make_async_remote_copy(
            src_ref=src,
            dst_ref=dst,
            send_sem=self.send_sems.at[index],
            recv_sem=self.recv_sems.at[index],
            device_id=device,
            device_id_type=pl.DeviceIdType.MESH,
        )

    def send(self, ref, device, to=None):
        index = self.count
        assert index < COPIES
        self.count += 1
        copy = self._copy(index, ref, ref if to is None else to, device)
        copy.start()
        self.sent.append(copy)
        return index

    def arrive(self, index, ref):
        self._copy(index, ref, ref, self.anyone).wait_recv()

    def finish(self):
        for copy in self.sent:
            copy.wait_send()


def build_table(feats, table, first, last):
    gap = jnp.where(lax.broadcasted_iota(jnp.int32, (16, LANES), 0) == 15, 1.0, 0.0)

    def step(chunk, carry):
        at = pl.multiple_of(chunk * LANES, LANES)
        columns = feats[:, pl.ds(at, LANES)].astype(F32)
        table[pl.ds(at, LANES), :] = jnp.concatenate([columns, gap, columns, gap], axis=0).T
        return carry

    lax.fori_loop(first, last, step, 0, unroll=4)


def as_columns(rows):
    rows = rows.astype(F32)
    left = jnp.full((16 - rows.shape[0], LANES), float(RELATIONS), F32)
    return jnp.concatenate([rows, left], axis=0).T


def build_relations(rel, by_row):
    for chunk in range(by_row.shape[0] // LANES):
        by_row[chunk * LANES : (chunk + 1) * LANES, :] = as_columns(rel[:, chunk, :])


def eight_means(base, row, column, nbr, table, by_row, picked):
    tile = (8, LANES)
    half = (lax.broadcasted_iota(jnp.int32, tile, 1) // 64).astype(F32)
    ids = by_row[pl.ds(base, 8), :]
    for k in range(FANOUT_ONE):
        for i in range(8):
            source = nbr[k, row, column + i]
            picked[k * 8 + i : k * 8 + i + 1, :] = table[pl.ds(source, 1), :]
    zero = jnp.zeros(tile, F32)
    low, high = zero, zero
    for k in range(FANOUT_ONE):
        rows = picked[k * 8 : (k + 1) * 8, :]
        own = jnp.broadcast_to(ids[:, k : k + 1], tile)
        low = low + jnp.where(own == half, rows, 0.0)
        high = high + jnp.where(own == half + 2.0, rows, 0.0)

    def mean(total):
        first = jnp.broadcast_to(total[:, 63:64], tile)
        second = jnp.broadcast_to(total[:, 127:128], tile)
        return total / jnp.maximum(jnp.where(half == 0.0, first, second), 1.0)

    return mean(low), mean(high)


def gather_block(block, to, nbr, table, by_row, picked, slabs):
    row, start = block // 2, lax.rem(block, 2) * ROWS
    lane = lax.broadcasted_iota(jnp.int32, (16, LANES), 1)
    spare = lax.rem(lane, 64) >= 48

    def step(group, carry):
        at = pl.multiple_of(group * 16, 16)
        base = pl.multiple_of(block * ROWS + at, 16)
        pairs = [
            eight_means(base + n * 8, row, start + at + n * 8, nbr, table, by_row, picked.at[n])
            for n in range(2)
        ]
        own = table[pl.ds(base, 16), :]
        beside = (
            jnp.where(lane < 64, pltpu.roll(own, 48, 1), pltpu.roll(own, 32, 1)),
            pltpu.roll(own, 16, 1),
        )
        for side in range(2):
            both = jnp.concatenate([pair[side] for pair in pairs], axis=0)
            both = jnp.where(spare, beside[side], both)
            slabs[pl.ds(to + at, 16), side * LANES : (side + 1) * LANES] = both.astype(BF16)
        return carry

    lax.fori_loop(0, ROWS // 16, step, 0)


def build_counts(keys, counts, first_row):
    span = counts.shape[1]

    def some_rows(n, carry):
        at = pl.multiple_of(n * 16, 16)
        key = keys[pl.ds(at, 16), :]
        tiles = jnp.floor(key * (1.0 / LANES))
        lane = lax.broadcasted_iota(jnp.int32, (16, LANES), 1).astype(F32)
        tile_of, ones = [], []
        for k in range(FANOUT_TWO):
            column = jnp.broadcast_to(key[:, k : k + 1], (16, LANES))
            tile = jnp.broadcast_to(tiles[:, k : k + 1], (16, LANES))
            tile_of.append(tile.astype(BF16))
            ones.append(jnp.where(column - tile * LANES == lane, 1.0, 0.0).astype(BF16))
        zero = jnp.zeros((16, LANES), BF16)
        for r in range(RELATIONS):
            for c in range(span // LANES):
                label = jnp.full((16, LANES), r * (span // LANES) + c, BF16)
                parts = [
                    jnp.where(tile_of[k] == label, ones[k], zero) for k in range(FANOUT_TWO)
                ]
                while len(parts) > 1:
                    parts = [sum(parts[i : i + 2][1:], parts[i]) for i in range(0, len(parts), 2)]
                rows = pl.ds(r * SIDE * ROWS + first_row + at, 16)
                counts[rows, c * LANES : (c + 1) * LANES] = parts[0]
        return carry

    lax.fori_loop(0, ROWS // 16, some_rows, 0)


def kernel(
    nbr_hbm,
    feats_hbm,
    rel_hbm,
    w_one_hbm,
    owner_hbm,
    within_hbm,
    ids_hbm,
    w_two,
    out,
    nbr,
    feats,
    rel,
    w_one,
    two,
    table,
    by_row,
    picked,
    slabs,
    columns_two,
    keys,
    counts,
    weights,
    hidden,
    send_right,
    send_left,
    from_left,
    from_right,
    summed,
    inverse,
    left_rows,
    accumulated,
    finished,
    arrived,
    send_sems,
    recv_sems,
    local_sems,
):
    z = lax.axis_index("feat")
    place = lax.axis_index("batch")
    core = lax.rem(place, 2)
    x = lax.rem(place // 2, SIDE)
    y = place // (2 * SIDE)
    u = x + core * (y - x)
    v = y + core * (x - y)
    z_high, z_low = z // SIDE, lax.rem(z, SIDE)

    def along(offset):
        return lax.rem(z + (FEAT + offset), FEAT)

    def turn(value, offset):
        return lax.rem(value + (SIDE + offset), SIDE)

    def in_plane(u_at, v_at):
        return (z, v_at * (8 - 6 * core) + u_at * (2 + 6 * core) + core)

    z_by = {d: (along(d), place) for d in (1, -1, 2, -2, 4, -4, 8)}
    u_by = {d: in_plane(turn(u, d), v) for d in (1, -1, 2)}
    v_by = {d: in_plane(u, turn(v, d)) for d in (1, -1, 2)}
    x_by = {d: (z, y * 2 * SIDE + turn(x, d) * 2 + core) for d in (1, -1, 2)}
    y_by = {d: (z, turn(y, d) * 2 * SIDE + x * 2 + core) for d in (1, -1, 2)}
    right, left = z_by[1], z_by[-1]
    peer = (z, place + 1 - 2 * core)

    wide = WIDTH // SIDE

    def lanes_of(which):
        return pl.ds(pl.multiple_of(which * LANES, LANES), LANES)

    here = pl.ds(pl.multiple_of(x * wide + core * LANES, LANES), LANES)

    chunks = 4
    span = feats.shape[1] // chunks
    copies = [
        (feats_hbm.at[:, pl.ds(n * span, span)], feats.at[:, pl.ds(n * span, span)])
        for n in range(chunks)
    ] + [
        (w_two.at[:, y, :, here], weights.at[:, z_high, z_low, y, :, lanes_of(core)]),
        (nbr_hbm, nbr),
        (rel_hbm, rel),
        (w_one_hbm.at[pl.ds(1, RELATIONS)], w_one.at[:, pl.ds(0, 48)]),
        *(
            (w_one_hbm.at[pl.ds(0, 1), pl.ds(16 * n, 16)], w_one.at[pl.ds(n, 1), pl.ds(48, 16)])
            for n in range(3)
        ),
        (owner_hbm, two.at[0]),
        (within_hbm, two.at[1]),
        (ids_hbm, two.at[2]),
    ]
    copies = [
        pltpu.make_async_copy(src, dst, local_sems.at[n]) for n, (src, dst) in enumerate(copies)
    ]
    for copy in copies:
        copy.start()

    barrier = pltpu.get_barrier_semaphore()
    neighbours = [*z_by.values(), *u_by.values(), *v_by.values(), peer]
    for device in neighbours:
        pl.semaphore_signal(barrier, inc=1, device_id=device, device_id_type=pl.DeviceIdType.MESH)

    links = Links(send_sems, recv_sems, peer)

    def piece(z_low_at, y_at, high=None):
        high = slice(None) if high is None else high
        return weights.at[:, high, z_low_at, y_at, :, lanes_of(core)]

    def column_half(z_low_at, which):
        return weights.at[:, :, z_low_at, :, :, lanes_of(which)]

    first_half, last_half = pl.ds(0, SIDE // 2), pl.ds(SIDE // 2, SIDE // 2)
    sent = {}

    def z_far():
        copies[chunks].wait()
        for d in (4, -4, 8):
            sent["z", d] = links.send(piece(z_low, y, z_high), z_by[d])

    def z_near():
        for d in (4, -4, 8):
            links.arrive(sent["z", d], piece(z_low, y, along(-d) // SIDE))
        for d in (1, -1):
            sent["z", d] = links.send(piece(z_low, y), z_by[d])
        sent["z", 2] = links.send(piece(z_low, y, first_half), z_by[2])
        sent["z", -2] = links.send(piece(z_low, y, last_half), z_by[-2])

    def z_arrive(c):
        if c == 2:
            links.arrive(sent["z", 2], piece(turn(z_low, 2), y, first_half))
            links.arrive(sent["z", -2], piece(turn(z_low, 2), y, last_half))
        elif c:
            links.arrive(sent["z", -c], piece(turn(z_low, c), y))

    def y_step(c):
        z_arrive(c)
        for d in (1, -1):
            sent["y", c, d] = links.send(piece(turn(z_low, c), y), y_by[d])

    def y_far(c):
        at = turn(z_low, c)
        for d in (1, -1):
            links.arrive(sent["y", c, d], piece(at, turn(y, -d)))
        sent["y", c, 2] = links.send(piece(at, turn(y, -1), first_half), y_by[1])
        sent["y", c, -2] = links.send(piece(at, turn(y, 1), last_half), y_by[-1])

    def across_step(c):
        at = turn(z_low, c)
        links.arrive(sent["y", c, 2], piece(at, turn(y, 2), first_half))
        links.arrive(sent["y", c, -2], piece(at, turn(y, 2), last_half))
        sent["across", c] = links.send(column_half(at, core), peer)

    plan = {
        3: [(z_near,), (y_step, 0)],
        6: [(y_far, 0)],
        7: [(y_step, 1), (y_step, -1)],
        8: [(y_step, 2)],
        10: [(across_step, 0), (y_far, 1)],
        11: [(y_far, -1)],
        12: [(y_far, 2)],
        14: [(across_step, 1)],
        15: [(across_step, -1)],
        16: [(across_step, 2)],
    }

    def serve(slot):
        for action, *given in plan.get(slot, ()):
            action(*given)

    for n in range(chunks):
        copies[n].wait()
        build_table(feats, table, n * span // LANES, (n + 1) * span // LANES)
        if n == 1:
            pl.semaphore_wait(barrier, len(neighbours))
            z_far()
    for copy in copies[chunks + 1 :]:
        copy.wait()
    build_relations(rel, by_row)
    block_row = z // 2
    owner, within, ids = (
        as_columns(two[n, :, pl.ds(block_row, 1), :].reshape(FANOUT_TWO, LANES)) for n in range(3)
    )
    owner = owner.astype(jnp.int32)
    parity, across_x, across_y = owner % 2, (owner // 2) % SIDE, owner // (2 * SIDE)
    held = across_y * SIDE + across_x + parity * (
        SIDE * SIDE + (SIDE - 1) * across_x - (SIDE - 1) * across_y
    )
    columns_two[...] = ids * float(BATCHES * ROWS) + held.astype(F32) * float(ROWS) + within
    mine = pl.ds(pl.multiple_of(lax.rem(z, 2) * ROWS, ROWS), ROWS)
    none = jnp.full((ROWS, LANES - 16), float(RELATIONS * BATCHES * ROWS), F32)
    keys[x] = jnp.concatenate([columns_two[mine, :], none], axis=1)
    for d in (1, -1, 2):
        sent["keys", d] = links.send(keys.at[x], x_by[d])
    w_one[3, 48:64, :] = jnp.zeros((16, WIDTH), BF16)

    def count(d):
        n = turn(x, -d)
        if d:
            links.arrive(sent["keys", d], keys.at[n])
        build_counts(keys.at[n], counts, n * ROWS)
        key = keys[n]
        for r in range(RELATIONS):
            low, high = float(r * BATCHES * ROWS), float((r + 1) * BATCHES * ROWS)
            inside = jnp.where((key >= low) & (key < high), 1.0, 0.0)
            number = jnp.maximum(jnp.sum(inside, axis=1, keepdims=True), 1.0)
            some = pl.ds(pl.multiple_of(r * SIDE * ROWS + n * ROWS, ROWS), ROWS)
            inverse[some, :] = jnp.broadcast_to(1.0 / number, (ROWS, LANES))

    in_right, in_left = {}, {}
    steps = FEAT // 2
    quarter = WIDTH // 4
    for s in range(steps + 1):
        gather_block(along(steps - s), 0, nbr, table, by_row, picked, slabs)
        serve(2 * s)
        if 0 < s < steps:
            gather_block(along(s - steps), ROWS, nbr, table, by_row, picked, slabs)
        serve(2 * s + 1)
        if s == steps:
            count(0)
            count(1)
        rows = 2 * ROWS if 0 < s < steps else ROWS
        for h in range(4):
            columns = slice(h * quarter, (h + 1) * quarter)
            partial = jnp.dot(
                slabs[0:rows, :],
                w_one[:, :, columns].reshape(RELATIONS * 64, quarter),
                preferred_element_type=F32,
            )
            if s == 0:
                if h < 2:
                    send_right[0, h] = partial.astype(BF16)
                    in_right[0, h] = links.send(send_right.at[0, h], right, from_left.at[0, h])
                else:
                    send_left[0, h] = partial.astype(BF16)
                    in_left[0, h] = links.send(send_left.at[0, h], left, from_right.at[0, h])
                continue
            if s == steps:
                links.arrive(in_right[s - 1, h], from_left.at[s - 1, h])
                links.arrive(in_left[s - 1, h], from_right.at[s - 1, h])
                total = partial + from_left[s - 1, h].astype(F32) + from_right[s - 1, h].astype(F32)
                hidden[core, v, u, :, columns] = jnp.maximum(total, 0.0).astype(BF16)
                continue
            onward, back = partial[:ROWS], partial[ROWS:]
            if (s - 1, h) in in_right:
                links.arrive(in_right[s - 1, h], from_left.at[s - 1, h])
                onward = onward + from_left[s - 1, h].astype(F32)
            send_right[s, h] = onward.astype(BF16)
            in_right[s, h] = links.send(send_right.at[s, h], right, from_left.at[s, h])
            if (s - 1, h) in in_left:
                links.arrive(in_left[s - 1, h], from_right.at[s - 1, h])
                back = back + from_right[s - 1, h].astype(F32)
            send_left[s, h] = back.astype(BF16)
            in_left[s, h] = links.send(send_left.at[s, h], left, from_right.at[s, h])

    def rows_of(du, dv):
        return hidden.at[core, turn(v, dv), turn(u, du)]

    def rows_of_peer(du, dv):
        return hidden.at[1 - core, turn(u, dv), turn(v, du)]

    order = (0, -1, 1, 2)
    crossed = {}

    def cross(du, dv):
        crossed[du, dv] = links.send(rows_of(du, dv), peer)

    def to_v(du):
        for d in (1, -1, 2) if du == 2 else (1, -1):
            sent["h", du, d] = links.send(rows_of(du, 0), v_by[d])

    def half_of(ref, which):
        return ref.at[pl.ds(which * (ROWS // 2), ROWS // 2)]

    def from_v(du):
        for d in (1, -1):
            links.arrive(sent["h", du, d], rows_of(du, -d))
        if du != 2:
            sent["h", du, 2] = links.send(half_of(rows_of(du, -1), 0), v_by[1])
            sent["h", du, -2] = links.send(half_of(rows_of(du, 1), 1), v_by[-1])
        cross(du, -1)
        cross(du, 1)

    def from_v_far(du):
        if du == 2:
            links.arrive(sent["h", du, 2], rows_of(du, 2))
        else:
            links.arrive(sent["h", du, 2], half_of(rows_of(du, 2), 0))
            links.arrive(sent["h", du, -2], half_of(rows_of(du, 2), 1))
        cross(du, 2)

    def add_group(which, v_at, first=False):
        group = which * SIDE + v_at
        columns = pl.ds(pl.multiple_of(group * 2 * LANES, 2 * LANES), 2 * LANES)

        def step(n, carry):
            at = pl.ds(pl.multiple_of(n * 256, 256), 256)
            rows = hidden[which, v_at, :, :, at].reshape(SIDE * ROWS, 256)
            for r in range(RELATIONS):
                some = slice(r * SIDE * ROWS, (r + 1) * SIDE * ROWS)
                product = jnp.dot(counts[some, columns], rows, preferred_element_type=F32)
                summed[some, at] = product if first else summed[some, at] + product
            return carry

        lax.fori_loop(0, WIDTH // 256, step, 0)

    for d in (1, -1, 2):
        sent["hu", d] = links.send(rows_of(0, 0), u_by[d])
    to_v(0)
    cross(0, 0)

    for du in (-1, 1, 2):
        links.arrive(sent["hu", -du if du != 2 else 2], rows_of(du, 0))
        to_v(du)
        cross(du, 0)
    count(-1)
    from_v(0)
    count(2)
    add_group(core, v, first=True)
    for du in (-1, 1):
        from_v(du)
    for du in order:
        links.arrive(crossed[du, 0], rows_of_peer(du, 0))
    add_group(1 - core, u)
    from_v_far(0)
    from_v(2)
    add_group(core, turn(v, -1))
    from_v_far(2)
    from_v_far(-1)
    from_v_far(1)
    add_group(core, turn(v, 1))
    add_group(core, turn(v, 2))
    for c in (0, 1, -1, 2):
        links.arrive(sent["across", c], column_half(turn(z_low, c), 1 - core))

    def product(slab):
        w = weights[slab].reshape(WIDTH, wide)
        return jnp.dot(left_rows[slab], w, preferred_element_type=F32)

    for n in range(SIDE):
        own = hidden[core, y + core * (n - y), n + core * (y - n)]
        left_rows[0, n * ROWS : (n + 1) * ROWS, :] = own
    accumulated[...] = product(0)
    for dv in (-1, 1, 2):
        for du in order:
            links.arrive(crossed[du, dv], rows_of_peer(du, dv))
        add_group(1 - core, turn(u, dv))
    for r in range(RELATIONS):
        some = slice(r * SIDE * ROWS, (r + 1) * SIDE * ROWS)
        for c in range(WIDTH // LANES):
            columns = slice(c * LANES, (c + 1) * LANES)
            left_rows[r + 1, :, columns] = (summed[some, columns] * inverse[some, :]).astype(BF16)
        accumulated[...] += product(r + 1)
    finished[...] = jnp.maximum(accumulated[...], 0.0).astype(BF16).reshape(SIDE, ROWS, wide)
    for d in (1, -1, 2):
        sent["out", d] = links.send(finished.at[turn(x, d)], x_by[d], arrived.at[x])
    arrived[x] = finished[x]
    for d in (1, -1, 2):
        links.arrive(sent["out", d], arrived.at[turn(x, -d)])
    for n in range(SIDE):
        out[:, n * wide : (n + 1) * wide] = arrived[n]
    links.finish()


COPIES = 144


def two_layers(nbr, feats, rel, w_one, owner, within, ids, w_two):
    sources = feats.shape[1]
    dest = WIDTH
    half_steps = FEAT // 2
    travelling = pltpu.VMEM((half_steps, 4, ROWS, WIDTH // 4), BF16)
    return pl.pallas_call(
        kernel,
        out_shape=jax.ShapeDtypeStruct((ROWS, WIDTH), BF16),
        in_specs=[pl.BlockSpec(memory_space=pl.ANY)] * 8,
        out_specs=pl.BlockSpec(memory_space=pltpu.VMEM),
        scratch_shapes=[
            pltpu.SMEM(nbr.shape, jnp.int32),
            pltpu.VMEM(feats.shape, BF16),
            pltpu.VMEM(rel.shape, jnp.int32),
            pltpu.VMEM((RELATIONS, 64, WIDTH), BF16),
            pltpu.VMEM((3, *ids.shape), jnp.int32),
            pltpu.VMEM((sources, LANES), F32),
            pltpu.VMEM((dest, 16), F32),
            pltpu.VMEM((2, FANOUT_ONE * 8, LANES), F32),
            pltpu.VMEM((2 * ROWS, 2 * LANES), BF16),
            pltpu.VMEM((LANES, 16), F32),
            pltpu.VMEM((SIDE, ROWS, LANES), F32),
            pltpu.VMEM((RELATIONS * SIDE * ROWS, BATCHES * ROWS), BF16),
            pltpu.VMEM((RELATIONS + 1, SIDE, SIDE, SIDE, ROWS // SIDE, WIDTH // SIDE), BF16),
            pltpu.VMEM((2, SIDE, SIDE, ROWS, WIDTH), BF16),
            travelling,
            travelling,
            travelling,
            travelling,
            pltpu.VMEM((RELATIONS * SIDE * ROWS, WIDTH), F32),
            pltpu.VMEM((RELATIONS * SIDE * ROWS, LANES), F32),
            pltpu.VMEM((RELATIONS + 1, SIDE * ROWS, WIDTH), BF16),
            pltpu.VMEM((SIDE * ROWS, WIDTH // SIDE), F32),
            pltpu.VMEM((SIDE, ROWS, WIDTH // SIDE), BF16),
            pltpu.VMEM((SIDE, ROWS, WIDTH // SIDE), BF16),
            pltpu.SemaphoreType.DMA((COPIES,)),
            pltpu.SemaphoreType.DMA((COPIES,)),
            pltpu.SemaphoreType.DMA((14,)),
        ],
        compiler_params=pltpu.CompilerParams(
            vmem_limit_bytes=62 << 20, collective_id=0, has_side_effects=True
        ),
        cost_estimate=pl.CostEstimate(
            flops=2_400_000_000, bytes_accessed=4_000_000, transcendentals=0
        ),
        name="two_layers",
    )(nbr, feats, rel, w_one, owner, within, ids, w_two)


def body(feats, nbr_one, rel_one, w_one, owner_two, local_two, rel_two, w_two):
    def slots_first(array):
        return array.reshape(DEST_ROWS, LANES, FANOUT_TWO).transpose(2, 0, 1)

    out = two_layers(
        nbr_one[0].reshape(FANOUT_ONE, DEST_ROWS, LANES),
        feats[0],
        rel_one[0].reshape(FANOUT_ONE, DEST_ROWS, LANES),
        w_one,
        slots_first(owner_two[0, :, :, 0]),
        slots_first(local_two[0]),
        slots_first(rel_two[0]),
        w_two.reshape(RELATIONS + 1, SIDE, ROWS // SIDE, WIDTH),
    )
    return out[None]


def solution(mesh):
    in_specs = (
        P("batch", "feat", None),
        P("batch", None, None),
        P("batch", None, None),
        P(None, "feat", None),
        P("batch", None, None, None),
        P("batch", None, None),
        P("batch", None, None),
        P(None, "feat", None),
    )
    out_specs = P("batch", "feat", None)
    return jax.shard_map(body, mesh=mesh, in_specs=in_specs, out_specs=out_specs, check_vma=False)
```

```python
import jax
import jax.numpy as jnp
from jax import lax
from jax.experimental import pallas as pl
from jax.experimental.pallas import tpu as pltpu
from jax.sharding import PartitionSpec as P

RELATIONS = 4
FANOUT_ONE = 15
FANOUT_TWO = 10
ROWS = 64
LANES = 128
WIDTH = 1024
HALF = WIDTH // 2
FEAT = 16
SIDE = 4
BATCHES = 32
DEST_ROWS = 8
BF16 = jnp.bfloat16
F32 = jnp.float32


class Links:
    def __init__(self, send_sems, recv_sems, anyone):
        self.send_sems, self.recv_sems, self.anyone = send_sems, recv_sems, anyone
        self.count = 0
        self.sent = []

    def _copy(self, index, src, dst, device):
        return pltpu.make_async_remote_copy(
            src_ref=src,
            dst_ref=dst,
            send_sem=self.send_sems.at[index],
            recv_sem=self.recv_sems.at[index],
            device_id=device,
            device_id_type=pl.DeviceIdType.MESH,
        )

    def send(self, ref, device, to=None):
        index = self.count
        assert index < COPIES
        self.count += 1
        copy = self._copy(index, ref, ref if to is None else to, device)
        copy.start()
        self.sent.append(copy)
        return index

    def arrive(self, index, ref):
        self._copy(index, ref, ref, self.anyone).wait_recv()

    def finish(self):
        for copy in self.sent:
            copy.wait_send()


def build_table(feats, table, first, last):
    def step(chunk, carry):
        at = pl.multiple_of(chunk * LANES, LANES)
        columns = feats[:, pl.ds(at, LANES)].astype(F32)
        gap = jnp.zeros((LANES // 2 - columns.shape[0], LANES), F32)
        table[pl.ds(at, LANES), :] = jnp.concatenate([columns, gap, columns, gap], axis=0).T
        return carry

    lax.fori_loop(first, last, step, 0, unroll=4)


def as_columns(rows):
    rows = rows.astype(F32)
    left = jnp.full((16 - rows.shape[0], LANES), float(RELATIONS), F32)
    return jnp.concatenate([rows, left], axis=0).T


def build_relations(rel, by_row):
    for chunk in range(by_row.shape[0] // LANES):
        by_row[chunk * LANES : (chunk + 1) * LANES, :] = as_columns(rel[:, chunk, :])


def eight_means(base, row, column, nbr, table, by_row, picked):
    tile = (8, LANES)
    half = (lax.broadcasted_iota(jnp.int32, tile, 1) // 64).astype(F32)
    ids = by_row[pl.ds(base, 8), :]
    for k in range(FANOUT_ONE):
        for i in range(8):
            source = nbr[k, row, column + i]
            picked[k * 8 + i : k * 8 + i + 1, :] = table[pl.ds(source, 1), :]
    zero = jnp.zeros(tile, F32)
    low, high, low_count, high_count = zero, zero, zero, zero
    for k in range(FANOUT_ONE):
        rows = picked[k * 8 : (k + 1) * 8, :]
        own = jnp.broadcast_to(ids[:, k : k + 1], tile)
        in_low, in_high = own == half, own == half + 2.0
        low = low + jnp.where(in_low, rows, 0.0)
        high = high + jnp.where(in_high, rows, 0.0)
        low_count = low_count + jnp.where(in_low, 1.0, 0.0)
        high_count = high_count + jnp.where(in_high, 1.0, 0.0)
    return low / jnp.maximum(low_count, 1.0), high / jnp.maximum(high_count, 1.0)


def gather_block(block, to, nbr, table, by_row, picked, slabs):
    row, start = block // 2, lax.rem(block, 2) * ROWS

    def step(group, carry):
        at = pl.multiple_of(group * 16, 16)
        base = pl.multiple_of(block * ROWS + at, 16)
        pairs = [
            eight_means(base + n * 8, row, start + at + n * 8, nbr, table, by_row, picked.at[n])
            for n in range(2)
        ]
        for side in range(2):
            both = jnp.concatenate([pair[side] for pair in pairs], axis=0)
            slabs[pl.ds(to + at, 16), side * LANES : (side + 1) * LANES] = both.astype(BF16)
        return carry

    lax.fori_loop(0, ROWS // 16, step, 0)
    first = pl.multiple_of(block * ROWS, ROWS)
    slabs[to : to + ROWS, 2 * LANES :] = table[pl.ds(first, ROWS), :].astype(BF16)


def build_counts(keys, counts, first_row):
    span = counts.shape[1]

    def some_rows(n, carry):
        at = pl.multiple_of(n * 16, 16)
        key = keys[pl.ds(at, 16), :]
        spread = [jnp.broadcast_to(key[:, k : k + 1], (16, LANES)) for k in range(FANOUT_TWO)]
        lane = lax.broadcasted_iota(jnp.int32, (16, LANES), 1).astype(F32)
        for r in range(RELATIONS):
            for c in range(span // LANES):
                label = lane + float(r * span + c * LANES)
                total = jnp.zeros((16, LANES), F32)
                for k in range(FANOUT_TWO):
                    total = total + jnp.where(spread[k] == label, 1.0, 0.0)
                rows = pl.ds(r * SIDE * ROWS + first_row + at, 16)
                counts[rows, c * LANES : (c + 1) * LANES] = total.astype(BF16)
        return carry

    lax.fori_loop(0, ROWS // 16, some_rows, 0)


def kernel(
    nbr_hbm,
    feats_hbm,
    rel_hbm,
    w_one_hbm,
    owner_hbm,
    within_hbm,
    ids_hbm,
    w_two,
    out,
    nbr,
    feats,
    rel,
    w_one,
    two,
    table,
    by_row,
    picked,
    slabs,
    columns_two,
    keys,
    counts,
    weights,
    hidden,
    send_right,
    send_left,
    from_left,
    from_right,
    summed,
    inverse,
    left_rows,
    accumulated,
    finished,
    arrived,
    send_sems,
    recv_sems,
    local_sems,
):
    z = lax.axis_index("feat")
    place = lax.axis_index("batch")
    core = lax.rem(place, 2)
    x = lax.rem(place // 2, SIDE)
    y = place // (2 * SIDE)
    u = x + core * (y - x)
    v = y + core * (x - y)
    z_high, z_low = z // SIDE, lax.rem(z, SIDE)

    def along(offset):
        return lax.rem(z + (FEAT + offset), FEAT)

    def turn(value, offset):
        return lax.rem(value + (SIDE + offset), SIDE)

    def in_plane(u_at, v_at):
        return (z, v_at * (8 - 6 * core) + u_at * (2 + 6 * core) + core)

    z_by = {d: (along(d), place) for d in (1, -1, 2, -2, 4, -4, 8)}
    u_by = {d: in_plane(turn(u, d), v) for d in (1, -1, 2)}
    v_by = {d: in_plane(u, turn(v, d)) for d in (1, -1, 2)}
    x_by = {d: (z, y * 2 * SIDE + turn(x, d) * 2 + core) for d in (1, -1, 2)}
    y_by = {d: (z, turn(y, d) * 2 * SIDE + x * 2 + core) for d in (1, -1, 2)}
    right, left = z_by[1], z_by[-1]
    peer = (z, place + 1 - 2 * core)

    wide = WIDTH // SIDE

    def lanes_of(which):
        return pl.ds(pl.multiple_of(which * LANES, LANES), LANES)

    here = pl.ds(pl.multiple_of(x * wide + core * LANES, LANES), LANES)

    chunks = 4
    span = feats.shape[1] // chunks
    copies = [
        (feats_hbm.at[:, pl.ds(n * span, span)], feats.at[:, pl.ds(n * span, span)])
        for n in range(chunks)
    ] + [
        (w_two.at[:, y, :, here], weights.at[:, z_high, z_low, y, :, lanes_of(core)]),
        (nbr_hbm, nbr),
        (rel_hbm, rel),
        (w_one_hbm.at[pl.ds(1, RELATIONS)], w_one.at[pl.ds(0, RELATIONS), pl.ds(0, 48)]),
        (w_one_hbm.at[pl.ds(0, 1)], w_one.at[pl.ds(RELATIONS, 1), pl.ds(0, 48)]),
        (owner_hbm, two.at[0]),
        (within_hbm, two.at[1]),
        (ids_hbm, two.at[2]),
    ]
    copies = [
        pltpu.make_async_copy(src, dst, local_sems.at[n]) for n, (src, dst) in enumerate(copies)
    ]
    for copy in copies:
        copy.start()

    barrier = pltpu.get_barrier_semaphore()
    neighbours = [*z_by.values(), *u_by.values(), *v_by.values(), peer]
    for device in neighbours:
        pl.semaphore_signal(barrier, inc=1, device_id=device, device_id_type=pl.DeviceIdType.MESH)

    links = Links(send_sems, recv_sems, peer)

    def piece(z_low_at, y_at, high=None):
        high = slice(None) if high is None else high
        return weights.at[:, high, z_low_at, y_at, :, lanes_of(core)]

    def column_half(z_low_at, which):
        return weights.at[:, :, z_low_at, :, :, lanes_of(which)]

    first_half, last_half = pl.ds(0, SIDE // 2), pl.ds(SIDE // 2, SIDE // 2)
    sent = {}

    def z_far():
        copies[chunks].wait()
        for d in (4, -4, 8):
            sent["z", d] = links.send(piece(z_low, y, z_high), z_by[d])

    def z_near():
        for d in (4, -4, 8):
            links.arrive(sent["z", d], piece(z_low, y, along(-d) // SIDE))
        for d in (1, -1):
            sent["z", d] = links.send(piece(z_low, y), z_by[d])
        sent["z", 2] = links.send(piece(z_low, y, first_half), z_by[2])
        sent["z", -2] = links.send(piece(z_low, y, last_half), z_by[-2])

    def z_arrive(c):
        if c == 2:
            links.arrive(sent["z", 2], piece(turn(z_low, 2), y, first_half))
            links.arrive(sent["z", -2], piece(turn(z_low, 2), y, last_half))
        elif c:
            links.arrive(sent["z", -c], piece(turn(z_low, c), y))

    def y_step(c):
        z_arrive(c)
        for d in (1, -1):
            sent["y", c, d] = links.send(piece(turn(z_low, c), y), y_by[d])

    def y_far(c):
        at = turn(z_low, c)
        for d in (1, -1):
            links.arrive(sent["y", c, d], piece(at, turn(y, -d)))
        sent["y", c, 2] = links.send(piece(at, turn(y, -1), first_half), y_by[1])
        sent["y", c, -2] = links.send(piece(at, turn(y, 1), last_half), y_by[-1])

    def across_step(c):
        at = turn(z_low, c)
        links.arrive(sent["y", c, 2], piece(at, turn(y, 2), first_half))
        links.arrive(sent["y", c, -2], piece(at, turn(y, 2), last_half))
        sent["across", c] = links.send(column_half(at, core), peer)

    plan = {
        3: [(z_near,), (y_step, 0)],
        6: [(y_far, 0)],
        7: [(y_step, 1), (y_step, -1)],
        8: [(y_step, 2)],
        10: [(across_step, 0), (y_far, 1)],
        11: [(y_far, -1)],
        12: [(y_far, 2)],
        14: [(across_step, 1)],
        15: [(across_step, -1)],
        16: [(across_step, 2)],
    }

    def serve(slot):
        for action, *given in plan.get(slot, ()):
            action(*given)

    for n in range(chunks):
        copies[n].wait()
        build_table(feats, table, n * span // LANES, (n + 1) * span // LANES)
        if n == 1:
            pl.semaphore_wait(barrier, len(neighbours))
            z_far()
    for copy in copies[chunks + 1 :]:
        copy.wait()
    build_relations(rel, by_row)
    block_row = z // 2
    owner, within, ids = (
        as_columns(two[n, :, pl.ds(block_row, 1), :].reshape(FANOUT_TWO, LANES)) for n in range(3)
    )
    owner = owner.astype(jnp.int32)
    parity, across_x, across_y = owner % 2, (owner // 2) % SIDE, owner // (2 * SIDE)
    held = across_y * SIDE + across_x + parity * (
        SIDE * SIDE + (SIDE - 1) * across_x - (SIDE - 1) * across_y
    )
    columns_two[...] = ids * float(BATCHES * ROWS) + held.astype(F32) * float(ROWS) + within
    mine = pl.ds(pl.multiple_of(lax.rem(z, 2) * ROWS, ROWS), ROWS)
    none = jnp.full((ROWS, LANES - 16), float(RELATIONS * BATCHES * ROWS), F32)
    keys[x] = jnp.concatenate([columns_two[mine, :], none], axis=1)
    for d in (1, -1, 2):
        sent["keys", d] = links.send(keys.at[x], x_by[d])
    w_one[:, 48:64, :] = jnp.zeros((6, 16, WIDTH), BF16)
    w_one[RELATIONS + 1, 0:48, :] = jnp.zeros((48, WIDTH), BF16)

    def count(d):
        n = turn(x, -d)
        if d:
            links.arrive(sent["keys", d], keys.at[n])
        build_counts(keys.at[n], counts, n * ROWS)
        key = keys[n]
        for r in range(RELATIONS):
            low, high = float(r * BATCHES * ROWS), float((r + 1) * BATCHES * ROWS)
            inside = jnp.where((key >= low) & (key < high), 1.0, 0.0)
            number = jnp.maximum(jnp.sum(inside, axis=1, keepdims=True), 1.0)
            some = pl.ds(pl.multiple_of(r * SIDE * ROWS + n * ROWS, ROWS), ROWS)
            inverse[some, :] = jnp.broadcast_to(1.0 / number, (ROWS, LANES))

    in_right, in_left = {}, {}
    steps = FEAT // 2
    quarter = WIDTH // 4
    for s in range(steps + 1):
        gather_block(along(steps - s), 0, nbr, table, by_row, picked, slabs)
        serve(2 * s)
        if 0 < s < steps:
            gather_block(along(s - steps), ROWS, nbr, table, by_row, picked, slabs)
        serve(2 * s + 1)
        if s == steps:
            count(0)
            count(1)
        rows = 2 * ROWS if 0 < s < steps else ROWS
        for h in range(4):
            columns = slice(h * quarter, (h + 1) * quarter)
            partial = jnp.dot(
                slabs[0:rows, :],
                w_one[:, :, columns].reshape(6 * 64, quarter),
                preferred_element_type=F32,
            )
            if s == 0:
                if h < 2:
                    send_right[0, h] = partial.astype(BF16)
                    in_right[0, h] = links.send(send_right.at[0, h], right, from_left.at[0, h])
                else:
                    send_left[0, h] = partial.astype(BF16)
                    in_left[0, h] = links.send(send_left.at[0, h], left, from_right.at[0, h])
                continue
            if s == steps:
                links.arrive(in_right[s - 1, h], from_left.at[s - 1, h])
                links.arrive(in_left[s - 1, h], from_right.at[s - 1, h])
                total = partial + from_left[s - 1, h].astype(F32) + from_right[s - 1, h].astype(F32)
                hidden[core, v, u, :, columns] = jnp.maximum(total, 0.0).astype(BF16)
                continue
            onward, back = partial[:ROWS], partial[ROWS:]
            if (s - 1, h) in in_right:
                links.arrive(in_right[s - 1, h], from_left.at[s - 1, h])
                onward = onward + from_left[s - 1, h].astype(F32)
            send_right[s, h] = onward.astype(BF16)
            in_right[s, h] = links.send(send_right.at[s, h], right, from_left.at[s, h])
            if (s - 1, h) in in_left:
                links.arrive(in_left[s - 1, h], from_right.at[s - 1, h])
                back = back + from_right[s - 1, h].astype(F32)
            send_left[s, h] = back.astype(BF16)
            in_left[s, h] = links.send(send_left.at[s, h], left, from_right.at[s, h])

    def rows_of(du, dv):
        return hidden.at[core, turn(v, dv), turn(u, du)]

    def rows_of_peer(du, dv):
        return hidden.at[1 - core, turn(u, dv), turn(v, du)]

    order = (0, -1, 1, 2)
    crossed = {}

    def cross(du, dv):
        crossed[du, dv] = links.send(rows_of(du, dv), peer)

    def to_v(du):
        for d in (1, -1, 2) if du == 2 else (1, -1):
            sent["h", du, d] = links.send(rows_of(du, 0), v_by[d])

    def half_of(ref, which):
        return ref.at[pl.ds(which * (ROWS // 2), ROWS // 2)]

    def from_v(du):
        for d in (1, -1):
            links.arrive(sent["h", du, d], rows_of(du, -d))
        if du != 2:
            sent["h", du, 2] = links.send(half_of(rows_of(du, -1), 0), v_by[1])
            sent["h", du, -2] = links.send(half_of(rows_of(du, 1), 1), v_by[-1])
        cross(du, -1)
        cross(du, 1)

    def from_v_far(du):
        if du == 2:
            links.arrive(sent["h", du, 2], rows_of(du, 2))
        else:
            links.arrive(sent["h", du, 2], half_of(rows_of(du, 2), 0))
            links.arrive(sent["h", du, -2], half_of(rows_of(du, 2), 1))
        cross(du, 2)

    def add_rows(dv, first=False):
        for du in order:
            links.arrive(crossed[du, dv], rows_of_peer(du, dv))
        groups = ((core, turn(v, dv)), (1 - core, turn(u, dv)))

        def step(n, carry):
            at = pl.ds(pl.multiple_of(n * 256, 256), 256)
            rows = [hidden[which, group, :, :, at].reshape(SIDE * ROWS, 256) for which, group in groups]
            for r in range(RELATIONS):
                some = slice(r * SIDE * ROWS, (r + 1) * SIDE * ROWS)
                product = sum(
                    jnp.dot(
                        counts[some, pl.ds(pl.multiple_of((which * SIDE + group) * 256, 256), 256)],
                        block,
                        preferred_element_type=F32,
                    )
                    for (which, group), block in zip(groups, rows)
                )
                summed[some, at] = product if first else summed[some, at] + product
            return carry

        lax.fori_loop(0, WIDTH // 256, step, 0)

    for d in (1, -1, 2):
        sent["hu", d] = links.send(rows_of(0, 0), u_by[d])
    to_v(0)
    cross(0, 0)

    count(-1)
    count(2)
    for du in (-1, 1, 2):
        links.arrive(sent["hu", -du if du != 2 else 2], rows_of(du, 0))
        to_v(du)
        cross(du, 0)
    from_v(0)
    from_v(-1)
    from_v(1)
    add_rows(0, first=True)
    from_v_far(0)
    from_v(2)
    for du in (-1, 1, 2):
        from_v_far(du)
    add_rows(-1)
    add_rows(1)
    for c in (0, 1, -1, 2):
        links.arrive(sent["across", c], column_half(turn(z_low, c), 1 - core))

    def product(slab):
        w = weights[slab].reshape(WIDTH, wide)
        return jnp.dot(left_rows[slab], w, preferred_element_type=F32)

    for n in range(SIDE):
        own = hidden[core, y + core * (n - y), n + core * (y - n)]
        left_rows[0, n * ROWS : (n + 1) * ROWS, :] = own
    accumulated[...] = product(0)
    add_rows(2)
    for r in range(RELATIONS):
        some = slice(r * SIDE * ROWS, (r + 1) * SIDE * ROWS)
        for c in range(WIDTH // LANES):
            columns = slice(c * LANES, (c + 1) * LANES)
            left_rows[r + 1, :, columns] = (summed[some, columns] * inverse[some, :]).astype(BF16)
        accumulated[...] += product(r + 1)
    finished[...] = jnp.maximum(accumulated[...], 0.0).astype(BF16).reshape(SIDE, ROWS, wide)
    for d in (1, -1, 2):
        sent["out", d] = links.send(finished.at[turn(x, d)], x_by[d], arrived.at[x])
    arrived[x] = finished[x]
    for d in (1, -1, 2):
        links.arrive(sent["out", d], arrived.at[turn(x, -d)])
    for n in range(SIDE):
        out[:, n * wide : (n + 1) * wide] = arrived[n]
    links.finish()


COPIES = 144


def two_layers(nbr, feats, rel, w_one, owner, within, ids, w_two):
    sources = feats.shape[1]
    dest = WIDTH
    half_steps = FEAT // 2
    travelling = pltpu.VMEM((half_steps, 4, ROWS, WIDTH // 4), BF16)
    return pl.pallas_call(
        kernel,
        out_shape=jax.ShapeDtypeStruct((ROWS, WIDTH), BF16),
        in_specs=[pl.BlockSpec(memory_space=pl.ANY)] * 8,
        out_specs=pl.BlockSpec(memory_space=pltpu.VMEM),
        scratch_shapes=[
            pltpu.SMEM(nbr.shape, jnp.int32),
            pltpu.VMEM(feats.shape, BF16),
            pltpu.VMEM(rel.shape, jnp.int32),
            pltpu.VMEM((RELATIONS + 2, 64, WIDTH), BF16),
            pltpu.VMEM((3, *ids.shape), jnp.int32),
            pltpu.VMEM((sources, LANES), F32),
            pltpu.VMEM((dest, 16), F32),
            pltpu.VMEM((2, FANOUT_ONE * 8, LANES), F32),
            pltpu.VMEM((2 * ROWS, 3 * LANES), BF16),
            pltpu.VMEM((LANES, 16), F32),
            pltpu.VMEM((SIDE, ROWS, LANES), F32),
            pltpu.VMEM((RELATIONS * SIDE * ROWS, BATCHES * ROWS), BF16),
            pltpu.VMEM((RELATIONS + 1, SIDE, SIDE, SIDE, ROWS // SIDE, WIDTH // SIDE), BF16),
            pltpu.VMEM((2, SIDE, SIDE, ROWS, WIDTH), BF16),
            travelling,
            travelling,
            travelling,
            travelling,
            pltpu.VMEM((RELATIONS * SIDE * ROWS, WIDTH), F32),
            pltpu.VMEM((RELATIONS * SIDE * ROWS, LANES), F32),
            pltpu.VMEM((RELATIONS + 1, SIDE * ROWS, WIDTH), BF16),
            pltpu.VMEM((SIDE * ROWS, WIDTH // SIDE), F32),
            pltpu.VMEM((SIDE, ROWS, WIDTH // SIDE), BF16),
            pltpu.VMEM((SIDE, ROWS, WIDTH // SIDE), BF16),
            pltpu.SemaphoreType.DMA((COPIES,)),
            pltpu.SemaphoreType.DMA((COPIES,)),
            pltpu.SemaphoreType.DMA((12,)),
        ],
        compiler_params=pltpu.CompilerParams(
            vmem_limit_bytes=62 << 20, collective_id=0, has_side_effects=True
        ),
        cost_estimate=pl.CostEstimate(
            flops=2_400_000_000, bytes_accessed=4_000_000, transcendentals=0
        ),
        name="two_layers",
    )(nbr, feats, rel, w_one, owner, within, ids, w_two)


def body(feats, nbr_one, rel_one, w_one, owner_two, local_two, rel_two, w_two):
    def slots_first(array):
        return array.reshape(DEST_ROWS, LANES, FANOUT_TWO).transpose(2, 0, 1)

    out = two_layers(
        nbr_one[0].reshape(FANOUT_ONE, DEST_ROWS, LANES),
        feats[0],
        rel_one[0].reshape(FANOUT_ONE, DEST_ROWS, LANES),
        w_one,
        slots_first(owner_two[0, :, :, 0]),
        slots_first(local_two[0]),
        slots_first(rel_two[0]),
        w_two.reshape(RELATIONS + 1, SIDE, ROWS // SIDE, WIDTH),
    )
    return out[None]


def solution(mesh):
    in_specs = (
        P("batch", "feat", None),
        P("batch", None, None),
        P("batch", None, None),
        P(None, "feat", None),
        P("batch", None, None, None),
        P("batch", None, None),
        P("batch", None, None),
        P(None, "feat", None),
    )
    out_specs = P("batch", "feat", None)
    return jax.shard_map(body, mesh=mesh, in_specs=in_specs, out_specs=out_specs, check_vma=False)
```

```python
import jax
import jax.numpy as jnp
from jax import lax
from jax.experimental import pallas as pl
from jax.experimental.pallas import tpu as pltpu
from jax.sharding import PartitionSpec as P

RELATIONS = 4
FANOUT_ONE = 15
FANOUT_TWO = 10
ROWS = 64
LANES = 128
WIDTH = 1024
HALF = WIDTH // 2
FEAT = 16
SIDE = 4
BATCHES = 32
DEST_ROWS = 8
BF16 = jnp.bfloat16
F32 = jnp.float32


class Links:
    def __init__(self, send_sems, recv_sems, anyone):
        self.send_sems, self.recv_sems, self.anyone = send_sems, recv_sems, anyone
        self.count = 0
        self.sent = []

    def _copy(self, index, src, dst, device):
        return pltpu.make_async_remote_copy(
            src_ref=src,
            dst_ref=dst,
            send_sem=self.send_sems.at[index],
            recv_sem=self.recv_sems.at[index],
            device_id=device,
            device_id_type=pl.DeviceIdType.MESH,
        )

    def send(self, ref, device, to=None):
        index = self.count
        assert index < COPIES
        self.count += 1
        copy = self._copy(index, ref, ref if to is None else to, device)
        copy.start()
        self.sent.append(copy)
        return index

    def arrive(self, index, ref):
        self._copy(index, ref, ref, self.anyone).wait_recv()

    def finish(self):
        for copy in self.sent:
            copy.wait_send()


def build_table(feats, table, first, last):
    def step(chunk, carry):
        at = pl.multiple_of(chunk * LANES, LANES)
        columns = feats[:, pl.ds(at, LANES)].astype(F32)
        gap = jnp.zeros((LANES // 2 - columns.shape[0], LANES), F32)
        table[pl.ds(at, LANES), :] = jnp.concatenate([columns, gap, columns, gap], axis=0).T
        return carry

    lax.fori_loop(first, last, step, 0, unroll=4)


def as_columns(rows):
    rows = rows.astype(F32)
    left = jnp.full((16 - rows.shape[0], LANES), float(RELATIONS), F32)
    return jnp.concatenate([rows, left], axis=0).T


def build_relations(rel, by_row):
    for chunk in range(by_row.shape[0] // LANES):
        by_row[chunk * LANES : (chunk + 1) * LANES, :] = as_columns(rel[:, chunk, :])


def eight_means(base, row, column, nbr, table, by_row, picked):
    tile = (8, LANES)
    half = (lax.broadcasted_iota(jnp.int32, tile, 1) // 64).astype(F32)
    ids = by_row[pl.ds(base, 8), :]
    for k in range(FANOUT_ONE):
        for i in range(8):
            source = nbr[k, row, column + i]
            picked[k * 8 + i : k * 8 + i + 1, :] = table[pl.ds(source, 1), :]
    zero = jnp.zeros(tile, F32)
    low, high, low_count, high_count = zero, zero, zero, zero
    for k in range(FANOUT_ONE):
        rows = picked[k * 8 : (k + 1) * 8, :]
        own = jnp.broadcast_to(ids[:, k : k + 1], tile)
        in_low, in_high = own == half, own == half + 2.0
        low = low + jnp.where(in_low, rows, 0.0)
        high = high + jnp.where(in_high, rows, 0.0)
        low_count = low_count + jnp.where(in_low, 1.0, 0.0)
        high_count = high_count + jnp.where(in_high, 1.0, 0.0)
    return low / jnp.maximum(low_count, 1.0), high / jnp.maximum(high_count, 1.0)


def gather_block(block, to, nbr, table, by_row, picked, slabs):
    row, start = block // 2, lax.rem(block, 2) * ROWS

    def step(group, carry):
        at = pl.multiple_of(group * 16, 16)
        base = pl.multiple_of(block * ROWS + at, 16)
        pairs = [
            eight_means(base + n * 8, row, start + at + n * 8, nbr, table, by_row, picked.at[n])
            for n in range(2)
        ]
        for side in range(2):
            both = jnp.concatenate([pair[side] for pair in pairs], axis=0)
            slabs[pl.ds(to + at, 16), side * LANES : (side + 1) * LANES] = both.astype(BF16)
        return carry

    lax.fori_loop(0, ROWS // 16, step, 0)
    first = pl.multiple_of(block * ROWS, ROWS)
    slabs[to : to + ROWS, 2 * LANES :] = table[pl.ds(first, ROWS), :].astype(BF16)


def build_counts(keys, counts, first_row):
    span = counts.shape[1]

    def some_rows(n, carry):
        at = pl.multiple_of(n * 16, 16)
        key = keys[pl.ds(at, 16), :]
        spread = [jnp.broadcast_to(key[:, k : k + 1], (16, LANES)) for k in range(FANOUT_TWO)]
        lane = lax.broadcasted_iota(jnp.int32, (16, LANES), 1).astype(F32)
        for r in range(RELATIONS):
            for c in range(span // LANES):
                label = lane + float(r * span + c * LANES)
                total = jnp.zeros((16, LANES), F32)
                for k in range(FANOUT_TWO):
                    total = total + jnp.where(spread[k] == label, 1.0, 0.0)
                rows = pl.ds(r * SIDE * ROWS + first_row + at, 16)
                counts[rows, c * LANES : (c + 1) * LANES] = total.astype(BF16)
        return carry

    lax.fori_loop(0, ROWS // 16, some_rows, 0)


def kernel(
    nbr_hbm,
    feats_hbm,
    rel_hbm,
    w_one_hbm,
    owner_hbm,
    within_hbm,
    ids_hbm,
    w_two,
    out,
    nbr,
    feats,
    rel,
    w_one,
    two,
    table,
    by_row,
    picked,
    slabs,
    columns_two,
    keys,
    counts,
    weights,
    hidden,
    send_right,
    send_left,
    from_left,
    from_right,
    summed,
    near,
    inverse,
    left_rows,
    accumulated,
    finished,
    arrived,
    send_sems,
    recv_sems,
    local_sems,
):
    z = lax.axis_index("feat")
    place = lax.axis_index("batch")
    core = lax.rem(place, 2)
    x = lax.rem(place // 2, SIDE)
    y = place // (2 * SIDE)
    u = x + core * (y - x)
    v = y + core * (x - y)
    z_high, z_low = z // SIDE, lax.rem(z, SIDE)

    def along(offset):
        return lax.rem(z + (FEAT + offset), FEAT)

    def turn(value, offset):
        return lax.rem(value + (SIDE + offset), SIDE)

    def in_plane(u_at, v_at):
        return (z, v_at * (8 - 6 * core) + u_at * (2 + 6 * core) + core)

    z_by = {d: (along(d), place) for d in (1, -1, 2, -2, 4, -4, 8)}
    u_by = {d: in_plane(turn(u, d), v) for d in (1, -1, 2)}
    v_by = {d: in_plane(u, turn(v, d)) for d in (1, -1, 2)}
    x_by = {d: (z, y * 2 * SIDE + turn(x, d) * 2 + core) for d in (1, -1, 2)}
    y_by = {d: (z, turn(y, d) * 2 * SIDE + x * 2 + core) for d in (1, -1, 2)}
    right, left = z_by[1], z_by[-1]
    peer = (z, place + 1 - 2 * core)

    wide = WIDTH // SIDE

    def lanes_of(which):
        return pl.ds(pl.multiple_of(which * LANES, LANES), LANES)

    here = pl.ds(pl.multiple_of(x * wide + core * LANES, LANES), LANES)

    chunks = 4
    span = feats.shape[1] // chunks
    copies = [
        (feats_hbm.at[:, pl.ds(n * span, span)], feats.at[:, pl.ds(n * span, span)])
        for n in range(chunks)
    ] + [
        (w_two.at[:, y, :, here], weights.at[:, z_high, z_low, y, :, lanes_of(core)]),
        (nbr_hbm, nbr),
        (rel_hbm, rel),
        (w_one_hbm.at[pl.ds(1, RELATIONS)], w_one.at[pl.ds(0, RELATIONS), pl.ds(0, 48)]),
        (w_one_hbm.at[pl.ds(0, 1)], w_one.at[pl.ds(RELATIONS, 1), pl.ds(0, 48)]),
        (owner_hbm, two.at[0]),
        (within_hbm, two.at[1]),
        (ids_hbm, two.at[2]),
    ]
    copies = [
        pltpu.make_async_copy(src, dst, local_sems.at[n]) for n, (src, dst) in enumerate(copies)
    ]
    for copy in copies:
        copy.start()

    barrier = pltpu.get_barrier_semaphore()
    neighbours = [*z_by.values(), *u_by.values(), *v_by.values(), peer]
    for device in neighbours:
        pl.semaphore_signal(barrier, inc=1, device_id=device, device_id_type=pl.DeviceIdType.MESH)

    links = Links(send_sems, recv_sems, peer)

    def piece(z_low_at, y_at, high=None):
        high = slice(None) if high is None else high
        return weights.at[:, high, z_low_at, y_at, :, lanes_of(core)]

    def column_half(z_low_at, which):
        return weights.at[:, :, z_low_at, :, :, lanes_of(which)]

    first_half, last_half = pl.ds(0, SIDE // 2), pl.ds(SIDE // 2, SIDE // 2)
    sent = {}

    def z_far():
        copies[chunks].wait()
        for d in (4, -4, 8):
            sent["z", d] = links.send(piece(z_low, y, z_high), z_by[d])

    def z_near():
        for d in (4, -4, 8):
            links.arrive(sent["z", d], piece(z_low, y, along(-d) // SIDE))
        for d in (1, -1):
            sent["z", d] = links.send(piece(z_low, y), z_by[d])
        sent["z", 2] = links.send(piece(z_low, y, first_half), z_by[2])
        sent["z", -2] = links.send(piece(z_low, y, last_half), z_by[-2])

    def z_arrive(c):
        if c == 2:
            links.arrive(sent["z", 2], piece(turn(z_low, 2), y, first_half))
            links.arrive(sent["z", -2], piece(turn(z_low, 2), y, last_half))
        elif c:
            links.arrive(sent["z", -c], piece(turn(z_low, c), y))

    def y_step(c):
        z_arrive(c)
        for d in (1, -1):
            sent["y", c, d] = links.send(piece(turn(z_low, c), y), y_by[d])

    def y_far(c):
        at = turn(z_low, c)
        for d in (1, -1):
            links.arrive(sent["y", c, d], piece(at, turn(y, -d)))
        sent["y", c, 2] = links.send(piece(at, turn(y, -1), first_half), y_by[1])
        sent["y", c, -2] = links.send(piece(at, turn(y, 1), last_half), y_by[-1])

    def across_step(c):
        at = turn(z_low, c)
        links.arrive(sent["y", c, 2], piece(at, turn(y, 2), first_half))
        links.arrive(sent["y", c, -2], piece(at, turn(y, 2), last_half))
        sent["across", c] = links.send(column_half(at, core), peer)

    plan = {
        3: [(z_near,), (y_step, 0)],
        6: [(y_far, 0)],
        7: [(y_step, 1), (y_step, -1)],
        8: [(y_step, 2)],
        10: [(across_step, 0), (y_far, 1)],
        11: [(y_far, -1)],
        12: [(y_far, 2)],
        14: [(across_step, 1)],
        15: [(across_step, -1)],
        16: [(across_step, 2)],
    }

    def serve(slot):
        for action, *given in plan.get(slot, ()):
            action(*given)

    for n in range(chunks):
        copies[n].wait()
        build_table(feats, table, n * span // LANES, (n + 1) * span // LANES)
        if n == 1:
            pl.semaphore_wait(barrier, len(neighbours))
            z_far()
    for copy in copies[chunks + 1 :]:
        copy.wait()
    build_relations(rel, by_row)
    block_row = z // 2
    owner, within, ids = (
        as_columns(two[n, :, pl.ds(block_row, 1), :].reshape(FANOUT_TWO, LANES)) for n in range(3)
    )
    owner = owner.astype(jnp.int32)
    parity, across_x, across_y = owner % 2, (owner // 2) % SIDE, owner // (2 * SIDE)
    held = across_y * SIDE + across_x + parity * (
        SIDE * SIDE + (SIDE - 1) * across_x - (SIDE - 1) * across_y
    )
    columns_two[...] = ids * float(BATCHES * ROWS) + held.astype(F32) * float(ROWS) + within
    mine = pl.ds(pl.multiple_of(lax.rem(z, 2) * ROWS, ROWS), ROWS)
    none = jnp.full((ROWS, LANES - 16), float(RELATIONS * BATCHES * ROWS), F32)
    keys[x] = jnp.concatenate([columns_two[mine, :], none], axis=1)
    for d in (1, -1, 2):
        sent["keys", d] = links.send(keys.at[x], x_by[d])
    w_one[:, 48:64, :] = jnp.zeros((6, 16, WIDTH), BF16)
    w_one[RELATIONS + 1, 0:48, :] = jnp.zeros((48, WIDTH), BF16)

    in_right, in_left = {}, {}
    steps = FEAT // 2
    quarter = WIDTH // 4
    for s in range(steps + 1):
        gather_block(along(steps - s), 0, nbr, table, by_row, picked, slabs)
        serve(2 * s)
        if 0 < s < steps:
            gather_block(along(s - steps), ROWS, nbr, table, by_row, picked, slabs)
        serve(2 * s + 1)
        rows = 2 * ROWS if 0 < s < steps else ROWS
        for h in range(4):
            columns = slice(h * quarter, (h + 1) * quarter)
            partial = jnp.dot(
                slabs[0:rows, :],
                w_one[:, :, columns].reshape(6 * 64, quarter),
                preferred_element_type=F32,
            )
            if s == 0:
                if h < 2:
                    send_right[0, h] = partial.astype(BF16)
                    in_right[0, h] = links.send(send_right.at[0, h], right, from_left.at[0, h])
                else:
                    send_left[0, h] = partial.astype(BF16)
                    in_left[0, h] = links.send(send_left.at[0, h], left, from_right.at[0, h])
                continue
            if s == steps:
                links.arrive(in_right[s - 1, h], from_left.at[s - 1, h])
                links.arrive(in_left[s - 1, h], from_right.at[s - 1, h])
                total = partial + from_left[s - 1, h].astype(F32) + from_right[s - 1, h].astype(F32)
                hidden[0, 0, 0, :, columns] = jnp.maximum(total, 0.0).astype(BF16)
                continue
            onward, back = partial[:ROWS], partial[ROWS:]
            if (s - 1, h) in in_right:
                links.arrive(in_right[s - 1, h], from_left.at[s - 1, h])
                onward = onward + from_left[s - 1, h].astype(F32)
            send_right[s, h] = onward.astype(BF16)
            in_right[s, h] = links.send(send_right.at[s, h], right, from_left.at[s, h])
            if (s - 1, h) in in_left:
                links.arrive(in_left[s - 1, h], from_right.at[s - 1, h])
                back = back + from_right[s - 1, h].astype(F32)
            send_left[s, h] = back.astype(BF16)
            in_left[s, h] = links.send(send_left.at[s, h], left, from_right.at[s, h])

    def rows_of(du, dv, which=0):
        return hidden.at[{0: 0, 1: 1, -1: 2, 2: 3}[dv], which, du % SIDE]

    def rows_of_peer(du, dv):
        return rows_of(du, dv, 1)

    def opposite(d):
        return d if d == 2 else -d

    order = (0, -1, 1, 2)
    crossed = {}

    def cross(du, dv):
        crossed[du, dv] = links.send(rows_of(du, dv), peer, rows_of_peer(du, dv))

    def to_v(du):
        for d in (1, -1, 2) if du == 2 else (1, -1):
            sent["h", du, d] = links.send(rows_of(du, 0), v_by[d], rows_of(du, opposite(d)))

    def half_of(ref, which):
        return ref.at[pl.ds(which * (ROWS // 2), ROWS // 2)]

    def from_v(du):
        for d in (1, -1):
            links.arrive(sent["h", du, d], rows_of(du, -d))
        if du != 2:
            far = rows_of(du, 2)
            sent["h", du, 2] = links.send(half_of(rows_of(du, -1), 0), v_by[1], half_of(far, 0))
            sent["h", du, -2] = links.send(half_of(rows_of(du, 1), 1), v_by[-1], half_of(far, 1))
        cross(du, -1)
        cross(du, 1)

    def from_v_far(du):
        if du == 2:
            links.arrive(sent["h", du, 2], rows_of(du, 2))
        else:
            links.arrive(sent["h", du, 2], half_of(rows_of(du, 2), 0))
            links.arrive(sent["h", du, -2], half_of(rows_of(du, 2), 1))
        cross(du, 2)

    def add_rows(first, number):
        depth = 2 * SIDE * ROWS
        columns = slice(first * depth, (first + number) * depth)

        def step(n, carry):
            at = pl.ds(pl.multiple_of(n * 256, 256), 256)
            rows = hidden[first : first + number, :, :, :, at].reshape(number * depth, 256)
            for r in range(RELATIONS):
                some = slice(r * SIDE * ROWS, (r + 1) * SIDE * ROWS)
                value = jnp.dot(counts[some, columns], rows, preferred_element_type=F32)
                if first:
                    value = value + summed[some, at]
                if first + number < SIDE:
                    summed[some, at] = value
                else:
                    part = inverse[some, :]
                    scaled = value * jnp.concatenate([part, part], axis=1)
                    left_rows[r + 1, :, at] = scaled.astype(BF16)
            return carry

        lax.fori_loop(0, WIDTH // 256, step, 0)

    def peer_rows(dv):
        for du in order:
            links.arrive(crossed[du, dv], rows_of_peer(du, dv))

    for d in (1, -1, 2):
        sent["hu", d] = links.send(rows_of(0, 0), u_by[d], rows_of(opposite(d), 0))
    to_v(0)
    cross(0, 0)

    def count(d):
        n = turn(x, -d)
        if d:
            links.arrive(sent["keys", d], keys.at[n])
        key = keys[n].astype(jnp.int32)
        holder = (key >> 6) & 31
        same = (holder >> 4) == core
        v_off = (((holder >> 2) & 3) - jnp.where(same, v, u)) & 3
        u_off = ((holder & 3) - jnp.where(same, u, v)) & 3
        place_of = (v_off ^ (v_off >> 1)) * (2 * SIDE) + jnp.where(same, 0, SIDE) + u_off
        relation = key >> 11
        near[...] = (relation * (BATCHES * ROWS) + place_of * ROWS + (key & 63)).astype(F32)
        build_counts(near, counts, n * ROWS)
        for r in range(RELATIONS):
            inside = jnp.where(relation == r, 1.0, 0.0)
            number = jnp.maximum(jnp.sum(inside, axis=1, keepdims=True), 1.0)
            some = pl.ds(pl.multiple_of(r * SIDE * ROWS + n * ROWS, ROWS), ROWS)
            inverse[some, :] = jnp.broadcast_to(1.0 / number, (ROWS, LANES))

    count(0)
    count(1)
    for du in (-1, 1, 2):
        links.arrive(sent["hu", -du if du != 2 else 2], rows_of(du, 0))
        to_v(du)
        cross(du, 0)
    count(-1)
    from_v(0)
    count(2)
    from_v(-1)
    from_v(1)
    peer_rows(0)
    add_rows(0, 1)
    from_v_far(0)
    from_v(2)
    for du in (2, -1, 1):
        from_v_far(du)
    peer_rows(1)
    peer_rows(-1)
    add_rows(1, 2)
    for c in (0, 1, -1, 2):
        links.arrive(sent["across", c], column_half(turn(z_low, c), 1 - core))

    def product(slab):
        w = weights[slab].reshape(WIDTH, wide)
        return jnp.dot(left_rows[slab], w, preferred_element_type=F32)

    for n in range(SIDE):
        off = turn(n - x, 0)
        own = hidden[core * (off + (off // 2) * (5 - 2 * off)), 0, (1 - core) * off]
        left_rows[0, n * ROWS : (n + 1) * ROWS, :] = own
    accumulated[...] = product(0)
    peer_rows(2)
    add_rows(3, 1)
    for r in range(RELATIONS):
        accumulated[...] += product(r + 1)
    finished[...] = jnp.maximum(accumulated[...], 0.0).astype(BF16).reshape(SIDE, ROWS, wide)
    for d in (1, -1, 2):
        sent["out", d] = links.send(finished.at[turn(x, d)], x_by[d], arrived.at[x])
    arrived[x] = finished[x]
    for d in (1, -1, 2):
        links.arrive(sent["out", d], arrived.at[turn(x, -d)])
    for n in range(SIDE):
        out[:, n * wide : (n + 1) * wide] = arrived[n]
    links.finish()


COPIES = 144


def two_layers(nbr, feats, rel, w_one, owner, within, ids, w_two):
    sources = feats.shape[1]
    dest = WIDTH
    half_steps = FEAT // 2
    travelling = pltpu.VMEM((half_steps, 4, ROWS, WIDTH // 4), BF16)
    return pl.pallas_call(
        kernel,
        out_shape=jax.ShapeDtypeStruct((ROWS, WIDTH), BF16),
        in_specs=[pl.BlockSpec(memory_space=pl.ANY)] * 8,
        out_specs=pl.BlockSpec(memory_space=pltpu.VMEM),
        scratch_shapes=[
            pltpu.SMEM(nbr.shape, jnp.int32),
            pltpu.VMEM(feats.shape, BF16),
            pltpu.VMEM(rel.shape, jnp.int32),
            pltpu.VMEM((RELATIONS + 2, 64, WIDTH), BF16),
            pltpu.VMEM((3, *ids.shape), jnp.int32),
            pltpu.VMEM((sources, LANES), F32),
            pltpu.VMEM((dest, 16), F32),
            pltpu.VMEM((2, FANOUT_ONE * 8, LANES), F32),
            pltpu.VMEM((2 * ROWS, 3 * LANES), BF16),
            pltpu.VMEM((LANES, 16), F32),
            pltpu.VMEM((SIDE, ROWS, LANES), F32),
            pltpu.VMEM((RELATIONS * SIDE * ROWS, BATCHES * ROWS), BF16),
            pltpu.VMEM((RELATIONS + 1, SIDE, SIDE, SIDE, ROWS // SIDE, WIDTH // SIDE), BF16),
            pltpu.VMEM((SIDE, 2, SIDE, ROWS, WIDTH), BF16),
            travelling,
            travelling,
            travelling,
            travelling,
            pltpu.VMEM((RELATIONS * SIDE * ROWS, WIDTH), F32),
            pltpu.VMEM((ROWS, LANES), F32),
            pltpu.VMEM((RELATIONS * SIDE * ROWS, LANES), F32),
            pltpu.VMEM((RELATIONS + 1, SIDE * ROWS, WIDTH), BF16),
            pltpu.VMEM((SIDE * ROWS, WIDTH // SIDE), F32),
            pltpu.VMEM((SIDE, ROWS, WIDTH // SIDE), BF16),
            pltpu.VMEM((SIDE, ROWS, WIDTH // SIDE), BF16),
            pltpu.SemaphoreType.DMA((COPIES,)),
            pltpu.SemaphoreType.DMA((COPIES,)),
            pltpu.SemaphoreType.DMA((12,)),
        ],
        compiler_params=pltpu.CompilerParams(
            vmem_limit_bytes=62 << 20, collective_id=0, has_side_effects=True
        ),
        cost_estimate=pl.CostEstimate(
            flops=2_400_000_000, bytes_accessed=4_000_000, transcendentals=0
        ),
        name="two_layers",
    )(nbr, feats, rel, w_one, owner, within, ids, w_two)


def body(feats, nbr_one, rel_one, w_one, owner_two, local_two, rel_two, w_two):
    def slots_first(array):
        return array.reshape(DEST_ROWS, LANES, FANOUT_TWO).transpose(2, 0, 1)

    out = two_layers(
        nbr_one[0].reshape(FANOUT_ONE, DEST_ROWS, LANES),
        feats[0],
        rel_one[0].reshape(FANOUT_ONE, DEST_ROWS, LANES),
        w_one,
        slots_first(owner_two[0, :, :, 0]),
        slots_first(local_two[0]),
        slots_first(rel_two[0]),
        w_two.reshape(RELATIONS + 1, SIDE, ROWS // SIDE, WIDTH),
    )
    return out[None]


def solution(mesh):
    in_specs = (
        P("batch", "feat", None),
        P("batch", None, None),
        P("batch", None, None),
        P(None, "feat", None),
        P("batch", None, None, None),
        P("batch", None, None),
        P("batch", None, None),
        P(None, "feat", None),
    )
    out_specs = P("batch", "feat", None)
    return jax.shard_map(body, mesh=mesh, in_specs=in_specs, out_specs=out_specs, check_vma=False)
```

```python
import jax
import jax.numpy as jnp
from jax import lax
from jax.experimental import pallas as pl
from jax.experimental.pallas import tpu as pltpu
from jax.sharding import PartitionSpec as P

RELATIONS = 4
FANOUT_ONE = 15
FANOUT_TWO = 10
ROWS = 64
LANES = 128
WIDTH = 1024
HALF = WIDTH // 2
FEAT = 16
SIDE = 4
BATCHES = 32
DEST_ROWS = 8
BF16 = jnp.bfloat16
F32 = jnp.float32


class Links:
    def __init__(self, send_sems, recv_sems, anyone):
        self.send_sems, self.recv_sems, self.anyone = send_sems, recv_sems, anyone
        self.count = 0
        self.sent = []

    def _copy(self, index, src, dst, device):
        return pltpu.make_async_remote_copy(
            src_ref=src,
            dst_ref=dst,
            send_sem=self.send_sems.at[index],
            recv_sem=self.recv_sems.at[index],
            device_id=device,
            device_id_type=pl.DeviceIdType.MESH,
        )

    def send(self, ref, device, to=None):
        index = self.count
        assert index < COPIES
        self.count += 1
        copy = self._copy(index, ref, ref if to is None else to, device)
        copy.start()
        self.sent.append(copy)
        return index

    def arrive(self, index, ref):
        self._copy(index, ref, ref, self.anyone).wait_recv()

    def finish(self):
        for copy in self.sent:
            copy.wait_send()


def build_table(feats, table, first, last):
    def step(chunk, carry):
        at = pl.multiple_of(chunk * LANES, LANES)
        columns = feats[:, pl.ds(at, LANES)].astype(F32)
        gap = jnp.zeros((LANES // 2 - columns.shape[0], LANES), F32)
        table[pl.ds(at, LANES), :] = jnp.concatenate([columns, gap, columns, gap], axis=0).T
        return carry

    lax.fori_loop(first, last, step, 0, unroll=4)


def as_columns(rows):
    rows = rows.astype(F32)
    left = jnp.full((16 - rows.shape[0], LANES), float(RELATIONS), F32)
    return jnp.concatenate([rows, left], axis=0).T


def build_relations(rel, by_row):
    for chunk in range(by_row.shape[0] // LANES):
        by_row[chunk * LANES : (chunk + 1) * LANES, :] = as_columns(rel[:, chunk, :])


def eight_means(base, row, column, nbr, table, by_row, picked):
    tile = (8, LANES)
    half = (lax.broadcasted_iota(jnp.int32, tile, 1) // 64).astype(F32)
    ids = by_row[pl.ds(base, 8), :]
    for k in range(FANOUT_ONE):
        for i in range(8):
            source = nbr[k, row, column + i]
            picked[k * 8 + i : k * 8 + i + 1, :] = table[pl.ds(source, 1), :]
    zero = jnp.zeros(tile, F32)
    low, high, low_count, high_count = zero, zero, zero, zero
    for k in range(FANOUT_ONE):
        rows = picked[k * 8 : (k + 1) * 8, :]
        own = jnp.broadcast_to(ids[:, k : k + 1], tile)
        in_low, in_high = own == half, own == half + 2.0
        low = low + jnp.where(in_low, rows, 0.0)
        high = high + jnp.where(in_high, rows, 0.0)
        low_count = low_count + jnp.where(in_low, 1.0, 0.0)
        high_count = high_count + jnp.where(in_high, 1.0, 0.0)
    return low / jnp.maximum(low_count, 1.0), high / jnp.maximum(high_count, 1.0)


def gather_block(block, to, nbr, table, by_row, picked, slabs):
    row, start = block // 2, lax.rem(block, 2) * ROWS

    def step(group, carry):
        at = pl.multiple_of(group * 16, 16)
        base = pl.multiple_of(block * ROWS + at, 16)
        pairs = [
            eight_means(base + n * 8, row, start + at + n * 8, nbr, table, by_row, picked.at[n])
            for n in range(2)
        ]
        for side in range(2):
            both = jnp.concatenate([pair[side] for pair in pairs], axis=0)
            slabs[pl.ds(to + at, 16), side * LANES : (side + 1) * LANES] = both.astype(BF16)
        return carry

    lax.fori_loop(0, ROWS // 16, step, 0)
    first = pl.multiple_of(block * ROWS, ROWS)
    slabs[to : to + ROWS, 2 * LANES :] = table[pl.ds(first, ROWS), :].astype(BF16)


def build_counts(keys, counts, first_row):
    span = counts.shape[1]

    def some_rows(n, carry):
        at = pl.multiple_of(n * 16, 16)
        key = keys[pl.ds(at, 16), :]
        spread = [jnp.broadcast_to(key[:, k : k + 1], (16, LANES)) for k in range(FANOUT_TWO)]
        lane = lax.broadcasted_iota(jnp.int32, (16, LANES), 1).astype(F32)
        for r in range(RELATIONS):
            for c in range(span // LANES):
                label = lane + float(r * span + c * LANES)
                total = jnp.zeros((16, LANES), F32)
                for k in range(FANOUT_TWO):
                    total = total + jnp.where(spread[k] == label, 1.0, 0.0)
                rows = pl.ds(r * SIDE * ROWS + first_row + at, 16)
                counts[rows, c * LANES : (c + 1) * LANES] = total.astype(BF16)
        return carry

    lax.fori_loop(0, ROWS // 16, some_rows, 0)


def kernel(
    nbr_hbm,
    feats_hbm,
    rel_hbm,
    w_one_hbm,
    owner_hbm,
    within_hbm,
    ids_hbm,
    w_two,
    out,
    nbr,
    feats,
    rel,
    w_one,
    two,
    table,
    by_row,
    picked,
    slabs,
    columns_two,
    keys,
    counts,
    weights,
    hidden,
    send_right,
    send_left,
    from_left,
    from_right,
    summed,
    near,
    inverse,
    left_rows,
    accumulated,
    finished,
    arrived,
    send_sems,
    recv_sems,
    local_sems,
):
    z = lax.axis_index("feat")
    place = lax.axis_index("batch")
    core = lax.rem(place, 2)
    x = lax.rem(place // 2, SIDE)
    y = place // (2 * SIDE)
    u = x + core * (y - x)
    v = y + core * (x - y)
    z_high, z_low = z // SIDE, lax.rem(z, SIDE)

    def along(offset):
        return lax.rem(z + (FEAT + offset), FEAT)

    def turn(value, offset):
        return lax.rem(value + (SIDE + offset), SIDE)

    def in_plane(u_at, v_at):
        return (z, v_at * (8 - 6 * core) + u_at * (2 + 6 * core) + core)

    z_by = {d: (along(d), place) for d in (1, -1, 2, -2, 4, -4, 8)}
    u_by = {d: in_plane(turn(u, d), v) for d in (1, -1, 2)}
    v_by = {d: in_plane(u, turn(v, d)) for d in (1, -1, 2)}
    x_by = {d: (z, y * 2 * SIDE + turn(x, d) * 2 + core) for d in (1, -1, 2)}
    y_by = {d: (z, turn(y, d) * 2 * SIDE + x * 2 + core) for d in (1, -1, 2)}
    right, left = z_by[1], z_by[-1]
    peer = (z, place + 1 - 2 * core)

    wide = WIDTH // SIDE

    def lanes_of(which):
        return pl.ds(pl.multiple_of(which * LANES, LANES), LANES)

    here = pl.ds(pl.multiple_of(x * wide + core * LANES, LANES), LANES)

    chunks = 4
    span = feats.shape[1] // chunks
    copies = [
        (feats_hbm.at[:, pl.ds(n * span, span)], feats.at[:, pl.ds(n * span, span)])
        for n in range(chunks)
    ] + [
        (w_two.at[:, y, :, here], weights.at[:, z_high, z_low, y, :, lanes_of(core)]),
        (nbr_hbm, nbr),
        (rel_hbm, rel),
        (w_one_hbm.at[pl.ds(1, RELATIONS)], w_one.at[pl.ds(0, RELATIONS), pl.ds(0, 48)]),
        (w_one_hbm.at[pl.ds(0, 1)], w_one.at[pl.ds(RELATIONS, 1), pl.ds(0, 48)]),
        (owner_hbm, two.at[0]),
        (within_hbm, two.at[1]),
        (ids_hbm, two.at[2]),
    ]
    copies = [
        pltpu.make_async_copy(src, dst, local_sems.at[n]) for n, (src, dst) in enumerate(copies)
    ]
    for copy in copies:
        copy.start()

    barrier = pltpu.get_barrier_semaphore()
    neighbours = [*z_by.values(), *u_by.values(), *v_by.values(), peer]
    for device in neighbours:
        pl.semaphore_signal(barrier, inc=1, device_id=device, device_id_type=pl.DeviceIdType.MESH)

    links = Links(send_sems, recv_sems, peer)

    def piece(z_low_at, y_at, high=None):
        high = slice(None) if high is None else high
        return weights.at[:, high, z_low_at, y_at, :, lanes_of(core)]

    def column_half(z_low_at, which):
        return weights.at[:, :, z_low_at, :, :, lanes_of(which)]

    first_half, last_half = pl.ds(0, SIDE // 2), pl.ds(SIDE // 2, SIDE // 2)
    sent = {}

    def z_far():
        copies[chunks].wait()
        for d in (4, -4, 8):
            sent["z", d] = links.send(piece(z_low, y, z_high), z_by[d])

    def z_near():
        for d in (4, -4, 8):
            links.arrive(sent["z", d], piece(z_low, y, along(-d) // SIDE))
        for d in (1, -1):
            sent["z", d] = links.send(piece(z_low, y), z_by[d])
        sent["z", 2] = links.send(piece(z_low, y, first_half), z_by[2])
        sent["z", -2] = links.send(piece(z_low, y, last_half), z_by[-2])

    def z_arrive(c):
        if c == 2:
            links.arrive(sent["z", 2], piece(turn(z_low, 2), y, first_half))
            links.arrive(sent["z", -2], piece(turn(z_low, 2), y, last_half))
        elif c:
            links.arrive(sent["z", -c], piece(turn(z_low, c), y))

    def y_step(c):
        z_arrive(c)
        for d in (1, -1):
            sent["y", c, d] = links.send(piece(turn(z_low, c), y), y_by[d])

    def y_far(c):
        at = turn(z_low, c)
        for d in (1, -1):
            links.arrive(sent["y", c, d], piece(at, turn(y, -d)))
        sent["y", c, 2] = links.send(piece(at, turn(y, -1), first_half), y_by[1])
        sent["y", c, -2] = links.send(piece(at, turn(y, 1), last_half), y_by[-1])

    def across_step(c):
        at = turn(z_low, c)
        links.arrive(sent["y", c, 2], piece(at, turn(y, 2), first_half))
        links.arrive(sent["y", c, -2], piece(at, turn(y, 2), last_half))
        sent["across", c] = links.send(column_half(at, core), peer)

    plan = {
        3: [(z_near,), (y_step, 0)],
        6: [(y_far, 0)],
        7: [(y_step, 1), (y_step, -1)],
        8: [(y_step, 2)],
        10: [(y_far, 1)],
        11: [(y_far, -1)],
        12: [(y_far, 2)],
    }

    def serve(slot):
        for action, *given in plan.get(slot, ()):
            action(*given)

    for n in range(chunks):
        copies[n].wait()
        build_table(feats, table, n * span // LANES, (n + 1) * span // LANES)
        if n == 1:
            pl.semaphore_wait(barrier, len(neighbours))
            z_far()
    for copy in copies[chunks + 1 :]:
        copy.wait()
    build_relations(rel, by_row)
    block_row = z // 2
    owner, within, ids = (
        as_columns(two[n, :, pl.ds(block_row, 1), :].reshape(FANOUT_TWO, LANES)) for n in range(3)
    )
    owner = owner.astype(jnp.int32)
    parity, across_x, across_y = owner % 2, (owner // 2) % SIDE, owner // (2 * SIDE)
    held = across_y * SIDE + across_x + parity * (
        SIDE * SIDE + (SIDE - 1) * across_x - (SIDE - 1) * across_y
    )
    columns_two[...] = ids * float(BATCHES * ROWS) + held.astype(F32) * float(ROWS) + within
    mine = pl.ds(pl.multiple_of(lax.rem(z, 2) * ROWS, ROWS), ROWS)
    none = jnp.full((ROWS, LANES - 16), float(RELATIONS * BATCHES * ROWS), F32)
    keys[x] = jnp.concatenate([columns_two[mine, :], none], axis=1)
    for d in (1, -1, 2):
        sent["keys", d] = links.send(keys.at[x], x_by[d])
    w_one[:, 48:64, :] = jnp.zeros((6, 16, WIDTH), BF16)
    w_one[RELATIONS + 1, 0:48, :] = jnp.zeros((48, WIDTH), BF16)

    in_right, in_left = {}, {}
    steps = FEAT // 2
    quarter = WIDTH // 4
    for s in range(steps + 1):
        gather_block(along(steps - s), 0, nbr, table, by_row, picked, slabs)
        serve(2 * s)
        if 0 < s < steps:
            gather_block(along(s - steps), ROWS, nbr, table, by_row, picked, slabs)
        serve(2 * s + 1)
        rows = 2 * ROWS if 0 < s < steps else ROWS
        for h in range(4):
            columns = slice(h * quarter, (h + 1) * quarter)
            partial = jnp.dot(
                slabs[0:rows, :],
                w_one[:, :, columns].reshape(6 * 64, quarter),
                preferred_element_type=F32,
            )
            if s == 0:
                if h < 2:
                    send_right[0, h] = partial.astype(BF16)
                    in_right[0, h] = links.send(send_right.at[0, h], right, from_left.at[0, h])
                else:
                    send_left[0, h] = partial.astype(BF16)
                    in_left[0, h] = links.send(send_left.at[0, h], left, from_right.at[0, h])
                continue
            if s == steps:
                links.arrive(in_right[s - 1, h], from_left.at[s - 1, h])
                links.arrive(in_left[s - 1, h], from_right.at[s - 1, h])
                total = partial + from_left[s - 1, h].astype(F32) + from_right[s - 1, h].astype(F32)
                hidden[0, 0, 0, :, columns] = jnp.maximum(total, 0.0).astype(BF16)
                continue
            onward, back = partial[:ROWS], partial[ROWS:]
            if (s - 1, h) in in_right:
                links.arrive(in_right[s - 1, h], from_left.at[s - 1, h])
                onward = onward + from_left[s - 1, h].astype(F32)
            send_right[s, h] = onward.astype(BF16)
            in_right[s, h] = links.send(send_right.at[s, h], right, from_left.at[s, h])
            if (s - 1, h) in in_left:
                links.arrive(in_left[s - 1, h], from_right.at[s - 1, h])
                back = back + from_right[s - 1, h].astype(F32)
            send_left[s, h] = back.astype(BF16)
            in_left[s, h] = links.send(send_left.at[s, h], left, from_right.at[s, h])

    def rows_of(du, dv, which=0):
        return hidden.at[{0: 0, 1: 1, -1: 2, 2: 3}[dv], which, du % SIDE]

    def rows_of_peer(du, dv):
        return rows_of(du, dv, 1)

    def opposite(d):
        return d if d == 2 else -d

    order = (0, -1, 1, 2)
    crossed = {}

    def cross(du, dv):
        crossed[du, dv] = links.send(rows_of(du, dv), peer, rows_of_peer(du, dv))

    def to_v(du):
        for d in (1, -1, 2) if du == 2 else (1, -1):
            sent["h", du, d] = links.send(rows_of(du, 0), v_by[d], rows_of(du, opposite(d)))

    def half_of(ref, which):
        return ref.at[pl.ds(which * (ROWS // 2), ROWS // 2)]

    def from_v(du):
        for d in (1, -1):
            links.arrive(sent["h", du, d], rows_of(du, -d))
        if du != 2:
            far = rows_of(du, 2)
            sent["h", du, 2] = links.send(half_of(rows_of(du, -1), 0), v_by[1], half_of(far, 0))
            sent["h", du, -2] = links.send(half_of(rows_of(du, 1), 1), v_by[-1], half_of(far, 1))
        cross(du, -1)
        cross(du, 1)

    def from_v_far(du):
        if du == 2:
            links.arrive(sent["h", du, 2], rows_of(du, 2))
        else:
            links.arrive(sent["h", du, 2], half_of(rows_of(du, 2), 0))
            links.arrive(sent["h", du, -2], half_of(rows_of(du, 2), 1))
        cross(du, 2)

    def add_rows(first, number):
        depth = 2 * SIDE * ROWS
        columns = slice(first * depth, (first + number) * depth)

        def step(n, carry):
            at = pl.ds(pl.multiple_of(n * 256, 256), 256)
            rows = hidden[first : first + number, :, :, :, at].reshape(number * depth, 256)
            for r in range(RELATIONS):
                some = slice(r * SIDE * ROWS, (r + 1) * SIDE * ROWS)
                value = jnp.dot(counts[some, columns], rows, preferred_element_type=F32)
                if first:
                    value = value + summed[some, at]
                if first + number < SIDE:
                    summed[some, at] = value
                else:
                    part = inverse[some, :]
                    scaled = value * jnp.concatenate([part, part], axis=1)
                    left_rows[r + 1, :, at] = scaled.astype(BF16)
            return carry

        lax.fori_loop(0, WIDTH // 256, step, 0)

    def peer_rows(dv):
        for du in order:
            links.arrive(crossed[du, dv], rows_of_peer(du, dv))

    for d in (1, -1, 2):
        sent["hu", d] = links.send(rows_of(0, 0), u_by[d], rows_of(opposite(d), 0))
    to_v(0)
    cross(0, 0)

    def count(d):
        n = turn(x, -d)
        if d:
            links.arrive(sent["keys", d], keys.at[n])
        key = keys[n].astype(jnp.int32)
        holder = (key >> 6) & 31
        same = (holder >> 4) == core
        v_off = (((holder >> 2) & 3) - jnp.where(same, v, u)) & 3
        u_off = ((holder & 3) - jnp.where(same, u, v)) & 3
        place_of = (v_off ^ (v_off >> 1)) * (2 * SIDE) + jnp.where(same, 0, SIDE) + u_off
        relation = key >> 11
        near[...] = (relation * (BATCHES * ROWS) + place_of * ROWS + (key & 63)).astype(F32)
        build_counts(near, counts, n * ROWS)
        for r in range(RELATIONS):
            inside = jnp.where(relation == r, 1.0, 0.0)
            number = jnp.maximum(jnp.sum(inside, axis=1, keepdims=True), 1.0)
            some = pl.ds(pl.multiple_of(r * SIDE * ROWS + n * ROWS, ROWS), ROWS)
            inverse[some, :] = jnp.broadcast_to(1.0 / number, (ROWS, LANES))

    for c in (0, 1, -1, 2):
        across_step(c)
    count(0)
    count(1)
    for du in (-1, 1, 2):
        links.arrive(sent["hu", -du if du != 2 else 2], rows_of(du, 0))
        to_v(du)
        cross(du, 0)
    count(-1)
    from_v(0)
    count(2)
    from_v(-1)
    from_v(1)
    peer_rows(0)
    add_rows(0, 1)
    from_v_far(0)
    from_v(2)
    for du in (2, -1, 1):
        from_v_far(du)
    peer_rows(1)
    peer_rows(-1)
    add_rows(1, 2)
    for c in (0, 1, -1, 2):
        links.arrive(sent["across", c], column_half(turn(z_low, c), 1 - core))

    def product(slab):
        w = weights[slab].reshape(WIDTH, wide)
        return jnp.dot(left_rows[slab], w, preferred_element_type=F32)

    for n in range(SIDE):
        off = turn(n - x, 0)
        own = hidden[core * (off + (off // 2) * (5 - 2 * off)), 0, (1 - core) * off]
        left_rows[0, n * ROWS : (n + 1) * ROWS, :] = own
    accumulated[...] = product(0)
    peer_rows(2)
    add_rows(3, 1)
    for r in range(RELATIONS):
        accumulated[...] += product(r + 1)
    finished[...] = jnp.maximum(accumulated[...], 0.0).astype(BF16).reshape(SIDE, ROWS, wide)
    for d in (1, -1, 2):
        sent["out", d] = links.send(finished.at[turn(x, d)], x_by[d], arrived.at[x])
    arrived[x] = finished[x]
    for d in (1, -1, 2):
        links.arrive(sent["out", d], arrived.at[turn(x, -d)])
    for n in range(SIDE):
        out[:, n * wide : (n + 1) * wide] = arrived[n]
    links.finish()


COPIES = 144


def two_layers(nbr, feats, rel, w_one, owner, within, ids, w_two):
    sources = feats.shape[1]
    dest = WIDTH
    half_steps = FEAT // 2
    travelling = pltpu.VMEM((half_steps, 4, ROWS, WIDTH // 4), BF16)
    return pl.pallas_call(
        kernel,
        out_shape=jax.ShapeDtypeStruct((ROWS, WIDTH), BF16),
        in_specs=[pl.BlockSpec(memory_space=pl.ANY)] * 8,
        out_specs=pl.BlockSpec(memory_space=pltpu.VMEM),
        scratch_shapes=[
            pltpu.SMEM(nbr.shape, jnp.int32),
            pltpu.VMEM(feats.shape, BF16),
            pltpu.VMEM(rel.shape, jnp.int32),
            pltpu.VMEM((RELATIONS + 2, 64, WIDTH), BF16),
            pltpu.VMEM((3, *ids.shape), jnp.int32),
            pltpu.VMEM((sources, LANES), F32),
            pltpu.VMEM((dest, 16), F32),
            pltpu.VMEM((2, FANOUT_ONE * 8, LANES), F32),
            pltpu.VMEM((2 * ROWS, 3 * LANES), BF16),
            pltpu.VMEM((LANES, 16), F32),
            pltpu.VMEM((SIDE, ROWS, LANES), F32),
            pltpu.VMEM((RELATIONS * SIDE * ROWS, BATCHES * ROWS), BF16),
            pltpu.VMEM((RELATIONS + 1, SIDE, SIDE, SIDE, ROWS // SIDE, WIDTH // SIDE), BF16),
            pltpu.VMEM((SIDE, 2, SIDE, ROWS, WIDTH), BF16),
            travelling,
            travelling,
            travelling,
            travelling,
            pltpu.VMEM((RELATIONS * SIDE * ROWS, WIDTH), F32),
            pltpu.VMEM((ROWS, LANES), F32),
            pltpu.VMEM((RELATIONS * SIDE * ROWS, LANES), F32),
            pltpu.VMEM((RELATIONS + 1, SIDE * ROWS, WIDTH), BF16),
            pltpu.VMEM((SIDE * ROWS, WIDTH // SIDE), F32),
            pltpu.VMEM((SIDE, ROWS, WIDTH // SIDE), BF16),
            pltpu.VMEM((SIDE, ROWS, WIDTH // SIDE), BF16),
            pltpu.SemaphoreType.DMA((COPIES,)),
            pltpu.SemaphoreType.DMA((COPIES,)),
            pltpu.SemaphoreType.DMA((12,)),
        ],
        compiler_params=pltpu.CompilerParams(
            vmem_limit_bytes=62 << 20, collective_id=0, has_side_effects=True
        ),
        cost_estimate=pl.CostEstimate(
            flops=2_400_000_000, bytes_accessed=4_000_000, transcendentals=0
        ),
        name="two_layers",
    )(nbr, feats, rel, w_one, owner, within, ids, w_two)


def body(feats, nbr_one, rel_one, w_one, owner_two, local_two, rel_two, w_two):
    def slots_first(array):
        return array.reshape(DEST_ROWS, LANES, FANOUT_TWO).transpose(2, 0, 1)

    out = two_layers(
        nbr_one[0].reshape(FANOUT_ONE, DEST_ROWS, LANES),
        feats[0],
        rel_one[0].reshape(FANOUT_ONE, DEST_ROWS, LANES),
        w_one,
        slots_first(owner_two[0, :, :, 0]),
        slots_first(local_two[0]),
        slots_first(rel_two[0]),
        w_two.reshape(RELATIONS + 1, SIDE, ROWS // SIDE, WIDTH),
    )
    return out[None]


def solution(mesh):
    in_specs = (
        P("batch", "feat", None),
        P("batch", None, None),
        P("batch", None, None),
        P(None, "feat", None),
        P("batch", None, None, None),
        P("batch", None, None),
        P("batch", None, None),
        P(None, "feat", None),
    )
    out_specs = P("batch", "feat", None)
    return jax.shard_map(body, mesh=mesh, in_specs=in_specs, out_specs=out_specs, check_vma=False)
```
